32 devices in a mesh: groups: 2 (over x), shot: 16 (over z, y, core).
Axes of the slice: x: 2, y: 2, z: 4, core: 2. Of those that a mesh axis runs over, the one named last changes fastest.
Arguments:
- velocity: float32 [2048, 16, 256], P(('groups', 'shot')), parts along dimension 0, may hold values from 0.2 to 0.4
- accumulated: float32 [2048, 16, 256], P(('groups', 'shot')), parts along dimension 0, may hold values from 0.1 to 1
- aperture_tiles: int32 [32, 32], P(('groups', 'shot')), parts along dimension 0, may hold values from 0 to 1023, as said below
- source_cell: int32 [32], P(('groups', 'shot')), parts along dimension 0, may hold values from 0 to 131071
- wavelet: float32 [32, 2], P(('groups', 'shot')), parts along dimension 0, may hold values from -6 to 6
- start_field: float32 [32, 2, 32, 32, 128], P(('groups', 'shot')), parts along dimension 0, may hold values from -6 to 6
- receiver_cells: int32 [32, 8192], P(('groups', 'shot')), parts along dimension 0, may hold values from 0 to 131071
- observed: float32 [32, 2, 8192], P(('groups', 'shot')), parts along dimension 0, may hold values from -6 to 6
Outputs:
- new_velocity: float32 [2048, 16, 256], P(('groups', 'shot')), parts along dimension 0
- new_accumulated: float32 [2048, 16, 256], P(('groups', 'shot')), parts along dimension 0
The draws below stay inside these ranges and needn't reach their ends.
There are 2 independent parts, one for each index of `groups`. The reference program is written for one: setup_inputs(seed, part) draws one part's arguments, and reference() takes and returns one part's arrays. A program takes and returns all parts, laid end to end along the dimension named above; each array names one. Nothing has to cross between parts.
Inputs may be any that keep to these rules, and one draw needn't show every extreme that they name: `aperture_tiles`: each row names 32 distinct tile ids; the owner of a tile id is id // 64; a row names at most 4 tiles of one owner, and every row names exactly 4 tiles of some owner.
All inputs are finite; a program needn't handle non-finite values.
Results may differ from the reference program's by a relative error of at most 0.0001.
Values sent between devices are 32-bit elements; how exact they have to be, the bound alone decides.
No kernel may reach another device: no remote copies, remote signals or barrier semaphores. Data moves between devices by JAX's collectives and lax.ppermute only.
A program may use at most 192 MiB of HBM per device.

```python
import math
import jax
import jax.numpy as jnp
from jax import lax

TS = 16
AX = 2
AY = 2
AZ = 8
STEPS = 2
TILES_DEV = 64
NREC = 8192
APT = 32
CAP = 4
NTILES = 1024
BX = 32
BY = 32
BZ = 128
CELLS = 131072
N_SHOT = 16


def draw_aperture_tiles(key, part):
    key = jax.random.fold_in(key, 11)
    key_jitter, key_favour, key_forced, key_offset, key_shuffle = jax.random.split(key, 5)
    number_of_slots = N_SHOT * CAP
    slot_holder_device = jnp.arange(number_of_slots, dtype=jnp.int32) // CAP
    random_perturbation = jax.random.randint(key_jitter, (N_SHOT, number_of_slots), 0, 2 ** 19)
    preferred_choice = jax.random.randint(key_favour, (N_SHOT,), 0, 2 ** 18)
    compelled_pick = jax.random.randint(key_forced, (N_SHOT,), 0, N_SHOT)
    extra_score_boost = jnp.where(slot_holder_device[None, :] == compelled_pick[:, None], 2 ** 20, 0)
    ranking_scores = (random_perturbation + preferred_choice[slot_holder_device][None, :] + extra_score_boost) * number_of_slots + jnp.arange(number_of_slots, dtype=jnp.int32)[None, :]
    unused, chosen = lax.top_k(ranking_scores, APT)
    owners = chosen // CAP
    within = chosen % CAP
    offsets = jax.random.randint(key_offset, (N_SHOT, N_SHOT), 0, TILES_DEV)
    local_ids = (jnp.take_along_axis(offsets, owners, axis=1) + within) % TILES_DEV
    tile_ids = owners * TILES_DEV + local_ids
    shuffle_keys = jax.random.randint(key_shuffle, (N_SHOT, APT), 0, 2 ** 20) * APT + jnp.arange(APT, dtype=jnp.int32)[None, :]
    shuffle = jnp.argsort(shuffle_keys, axis=1)
    return jnp.take_along_axis(tile_ids, shuffle, axis=1).astype(jnp.int32)


def with_ends(drawn, key, low, high):
    shape = drawn.shape
    spot = [jax.random.randint(jax.random.fold_in(key, axis), (), 0, shape[axis]) for axis in range(len(shape))]
    drawn = drawn.at[tuple(spot)].set(low)
    longest = shape.index(max(shape))
    spot[longest] = (spot[longest] + 1) % shape[longest]
    return drawn.at[tuple(spot)].set(high)


def block_levels(key, extent, cuts, low, high):
    level, own = 1.0, jax.random.fold_in(key, 6)
    for position, parts in cuts:
        steps = jnp.exp(jax.random.uniform(jax.random.fold_in(own, position), (parts,), jnp.float32, low / len(cuts), high / len(cuts)))
        level = level * jnp.repeat(steps, extent[position] // parts).reshape([-1 if axis == position else 1 for axis in range(len(extent))])
    return level


def gaussian(key, shape, deviation, most, shards=(), kind=jnp.bfloat16):
    drawn = jax.random.normal(key, shape, jnp.float32) * deviation
    if len(shards) > 0:
        drawn = block_levels(key, shape, shards, -0.22, 0.18) * drawn
    return jnp.clip(drawn, min=-most, max=most).astype(kind)


def setup_inputs(seed: int = 0, part: int = 0) -> dict:
    key_of = jax.random.split(jax.random.key(seed), 9)
    own_keys = jax.random.split(jax.random.fold_in(key_of[8], part), 9)
    return {
        "velocity": jnp.clip(jnp.exp(math.log(0.4) - 0.6931472 * jax.random.uniform(own_keys[0], (NTILES, TS, TS * TS), jnp.float32) ** block_levels(own_keys[0], (NTILES, TS, TS * TS), ((0, 16),), -0.2, 0.2)), 0.2, 0.4),
        "accumulated": jnp.clip(jnp.exp(math.log(1.0) - 2.3025851 * jax.random.uniform(own_keys[1], (NTILES, TS, TS * TS), jnp.float32) ** block_levels(own_keys[1], (NTILES, TS, TS * TS), ((0, 16),), -0.2, 0.2)), 0.1, 1.0),
        "aperture_tiles": draw_aperture_tiles(jax.random.fold_in(jax.random.fold_in(key_of[8], part), 71), part),
        "source_cell": with_ends(jax.random.randint(own_keys[3], (N_SHOT,), 0, CELLS), jax.random.fold_in(own_keys[3], 1), 0, CELLS - 1).astype(jnp.int32),
        "wavelet": gaussian(own_keys[4], (N_SHOT, STEPS), 1.0, 6.0, ((0, 16),), jnp.float32),
        "start_field": gaussian(own_keys[5], (N_SHOT, 2, BX, BY, BZ), 1.0, 6.0, ((0, 16),), jnp.float32),
        "receiver_cells": with_ends(jax.random.randint(own_keys[6], (N_SHOT, NREC), 0, CELLS), jax.random.fold_in(own_keys[6], 1), 0, CELLS - 1).astype(jnp.int32),
        "observed": gaussian(own_keys[7], (N_SHOT, STEPS, NREC), 1.0, 6.0, ((0, 16),), jnp.float32),
    }


stencil_weights = (-205.0 / 72.0, 8.0 / 5.0, -1.0 / 5.0, 8.0 / 315.0, -1.0 / 560.0)
step_rate = 0.02

def laplacian(wavefield):
    cells_first, cells_second, cells_third = wavefield.shape
    padded = jnp.pad(wavefield, 4)
    running = 3.0 * stencil_weights[0] * wavefield
    for offset in range(1, 5):
        weight = stencil_weights[offset]
        pair_first = padded[4 + offset:4 + offset + cells_first, 4:4 + cells_second, 4:4 + cells_third] + padded[4 - offset:4 - offset + cells_first, 4:4 + cells_second, 4:4 + cells_third]
        pair_second = padded[4:4 + cells_first, 4 + offset:4 + offset + cells_second, 4:4 + cells_third] + padded[4:4 + cells_first, 4 - offset:4 - offset + cells_second, 4:4 + cells_third]
        pair_third = padded[4:4 + cells_first, 4:4 + cells_second, 4 + offset:4 + offset + cells_third] + padded[4:4 + cells_first, 4:4 + cells_second, 4 - offset:4 - offset + cells_third]
        running = running + weight * (pair_first + pair_second + pair_third)
    return running

def misfit(courant, initial, source_index, wavelet_row, receivers, recorded):
    squared = courant * courant
    previous = initial[0]
    current = initial[1]
    running = jnp.float32(0.0)
    for step_index in range(STEPS):
        future = 2.0 * current - previous + squared * laplacian(current)
        flat_field = future.reshape(-1).at[source_index].add(wavelet_row[step_index])
        mismatch = flat_field[receivers] - recorded[step_index]
        running = running + 0.5 * jnp.sum(mismatch * mismatch)
        previous = current
        current = flat_field.reshape(future.shape)
    return running

def assemble(tile_block):
    blocks = tile_block.reshape(AX, AY, AZ, TS, TS, TS)
    return blocks.transpose(0, 3, 1, 4, 2, 5).reshape(AX * TS, AY * TS, AZ * TS)

def disassemble(volume):
    blocks = volume.reshape(AX, TS, AY, TS, AZ, TS).transpose(0, 2, 4, 1, 3, 5)
    return blocks.reshape(AX * AY * AZ, TS, TS * TS)

def shot_gradient(tile_block, source_index, wavelet_row, initial, receivers, recorded):
    volume = assemble(tile_block)
    derivative = jax.grad(misfit)(volume, initial, source_index, wavelet_row, receivers, recorded)
    return disassemble(derivative)

def reference(velocity, accumulated, aperture_tiles, source_cell, wavelet, start_field, receiver_cells, observed):

    def one_shot(pooled, shot_index):
        tile_ids = aperture_tiles[shot_index]
        gradient_tiles = shot_gradient(velocity[tile_ids], source_cell[shot_index], wavelet[shot_index], start_field[shot_index], receiver_cells[shot_index], observed[shot_index])
        return (pooled.at[tile_ids].add(gradient_tiles), None)
    pooled, unused = lax.scan(one_shot, jnp.zeros(velocity.shape, jnp.float32), jnp.arange(N_SHOT, dtype=jnp.int32))
    new_accumulated = accumulated + pooled * pooled
    new_velocity = velocity - step_rate * pooled / jnp.sqrt(new_accumulated)
    return (new_velocity, new_accumulated)
```

```python
import functools

import jax
import jax.numpy as jnp
import numpy as np
from jax import lax
from jax.experimental import pallas as pl
from jax.experimental.pallas import tpu as pltpu
from jax.sharding import PartitionSpec as P

TS = 16
AX = 2
AY = 2
AZ = 8
BX = AX * TS
BY = AY * TS
APT = AX * AY * AZ
ROWS = BX * AZ
LANES = BY * TS
HALF = TS * TS
PAD = 4 * AZ
CHUNK = 512

scaled_weights = (-14350.0, 8064.0, -1008.0, 128.0, -9.0)
weight_scale = 1.0 / 5040.0
step_rate = 0.02


def stencil_matrices():
    lane = np.arange(LANES)
    y, l = lane // TS, lane % TS
    same = np.zeros((LANES, LANES), np.float32)
    cross = np.zeros((LANES, LANES), np.float32)
    for offset in range(1, 5):
        w = scaled_weights[offset]
        dy = np.abs(y[:, None] - y[None, :])
        dl = np.abs(l[:, None] - l[None, :])
        same += w * ((dl == 0) & (dy == offset))
        same += w * ((dy == 0) & (dl == offset))
        cross += w * ((dy == 0) & (dl == TS - offset))
    return same, cross[:HALF, :HALF]


def split(value):
    high = value.astype(jnp.bfloat16)
    rest = value - high.astype(jnp.float32)
    middle = rest.astype(jnp.bfloat16)
    low = (rest - middle.astype(jnp.float32)).astype(jnp.bfloat16)
    return high, middle, low


def stencil_products(field, parts, near, far, same_ref, cross_ref):
    for row in range(0, ROWS, 16):
        pieces = split(field[PAD + row : PAD + row + 16, :])
        for p in range(3):
            parts[p, row : row + 16, :] = pieces[p]
    same = same_ref[...]
    cross = cross_ref[...]
    dot = functools.partial(jnp.dot, preferred_element_type=jnp.float32)
    near[...] = dot(parts[0], same) + dot(parts[1], same) + dot(parts[2], same)
    for side in range(0, LANES, HALF):
        cols = slice(side, side + HALF)
        far[:, cols] = (
            dot(parts[0, :, cols], cross) + dot(parts[1, :, cols], cross) + dot(parts[2, :, cols], cross)
        )


def laplacian_rows(field, near, far, row, upper, keep):
    at = PAD + row
    total = near[row : row + AZ, :] + 3.0 * scaled_weights[0] * field[at : at + AZ, :]
    for offset in range(1, 5):
        above = field[at + offset * AZ : at + offset * AZ + AZ, :]
        below = field[at - offset * AZ : at - offset * AZ + AZ, :]
        total = total + scaled_weights[offset] * (above + below)
    other = far[row : row + AZ, :]
    moved = jnp.where(upper, pltpu.roll(other, AZ - 1, 0), pltpu.roll(other, 1, 0))
    return weight_scale * (total + jnp.where(keep, moved, 0.0))


def far_masks():
    lane = lax.broadcasted_iota(jnp.int32, (AZ, LANES), 1) % TS
    row = lax.broadcasted_iota(jnp.int32, (AZ, LANES), 0)
    upper = lane >= TS // 2
    keep = row != jnp.where(upper, AZ - 1, 0)
    return upper, keep


def clear_pads(field):
    zero = jnp.zeros((PAD, LANES), jnp.float32)
    field[:PAD, :] = zero
    field[PAD + ROWS :, :] = zero


def request_kernel(capacity, per_device, ids, table, slots, counts):
    devices = table.shape[0]
    for owner in range(devices):
        counts[owner] = 0
    owner_of = lax.broadcasted_iota(jnp.int32, table.shape, 0)
    rank_of = lax.broadcasted_iota(jnp.int32, table.shape, 1)
    position = owner_of * capacity + jnp.where(rank_of < capacity, rank_of, -devices * capacity)
    found = jnp.full(table.shape, -1, jnp.int32)
    for k in range(APT):
        tile = ids[0, k]
        owner = tile // per_device
        rank = counts[owner]
        counts[owner] = rank + 1
        slot = owner * capacity + rank
        slots[0, k] = slot
        found = jnp.where(position == slot, tile - owner * per_device, found)
    table[...] = found


def gather_kernel(capacity, wanted, velocity, outgoing):
    devices = wanted.shape[0]

    def step(shot, carry):
        for rank in range(capacity):
            tile = jnp.maximum(wanted[shot, rank], 0)
            outgoing[shot * capacity + rank] = velocity[tile]
        return carry

    lax.fori_loop(0, devices, step, 0, unroll=4)


def prepare_kernel(source, wavelet, start, same_ref, cross_ref, lap0, base1, base2, field, parts, near, far):
    clear_pads(field)
    cell = source[0]
    sx, sy, sz = cell // (BY * AZ * TS), (cell // (AZ * TS)) % BY, cell % (AZ * TS)
    source_row = sx * AZ + sz // TS
    source_lane = sy * TS + sz % TS
    lane = lax.broadcasted_iota(jnp.int32, (8, 128), 1)
    sub = lax.broadcasted_iota(jnp.int32, (8, 128), 0)
    wide_lane = lax.broadcasted_iota(jnp.int32, (AZ, LANES), 1)
    wide_row = lax.broadcasted_iota(jnp.int32, (AZ, LANES), 0)

    def turn(block):
        for bit in (1, 2, 4):
            sub_bit = sub & bit
            lane_bit = (lane // TS) & bit
            up = pltpu.roll(pltpu.roll(block, 8 - bit, 0), bit * TS, 1)
            down = pltpu.roll(pltpu.roll(block, bit, 0), 128 - bit * TS, 1)
            block = jnp.where(sub_bit == lane_bit, block, jnp.where(lane_bit != 0, up, down))
        return block

    for x in range(BX):
        hit = (wide_row == source_row - x * AZ) & (wide_lane == source_lane)
        previous = jnp.concatenate([turn(start[0, x, y : y + 8, :]) for y in range(0, BY, 8)], axis=1)
        current = jnp.concatenate([turn(start[1, x, y : y + 8, :]) for y in range(0, BY, 8)], axis=1)
        rows = slice(x * AZ, x * AZ + AZ)
        field[PAD + x * AZ : PAD + x * AZ + AZ, :] = current
        base1[rows, :] = 2.0 * current - previous + jnp.where(hit, wavelet[0, 0], 0.0)
        base2[rows, :] = jnp.where(hit, wavelet[0, 1], 0.0) - current
    stencil_products(field, parts, near, far, same_ref, cross_ref)
    upper, keep = far_masks()
    for x in range(BX):
        lap0[x * AZ : x * AZ + AZ, :] = laplacian_rows(field, near, far, x * AZ, upper, keep)


def receivers_kernel(cells, recorded, counts, sums0, sums1, left, right):
    step = pl.program_id(0)
    here = pl.ds(pl.multiple_of(step * CHUNK, CHUNK), CHUNK)
    cell = cells[:, here]
    x, y, z = cell // (BY * AZ * TS), (cell // (AZ * TS)) % BY, cell % (AZ * TS)
    row = x * AZ + z // TS
    lane = y * TS + z % TS
    row_hot = jnp.where(lax.broadcasted_iota(jnp.int32, (ROWS, CHUNK), 0) == row, 1.0, 0.0).astype(jnp.bfloat16)
    right[...] = jnp.where(lax.broadcasted_iota(jnp.int32, (LANES, CHUNK), 0) == lane, 1.0, 0.0).astype(jnp.bfloat16)
    left[:ROWS, :] = row_hot
    for n in range(2):
        pieces = split(jnp.broadcast_to(recorded[n : n + 1, here], (16, CHUNK)))
        for p in range(3):
            at = (1 + 3 * n + p) * ROWS
            left[at : at + ROWS, :] = (row_hot.reshape(ROWS // 16, 16, CHUNK) * pieces[p][None]).reshape(ROWS, CHUNK)

    @pl.when(step == 0)
    def _():
        for ref in (counts, sums0, sums1):
            ref[...] = jnp.zeros_like(ref)

    def hits(part):
        return lax.dot_general(
            left[part * ROWS : (part + 1) * ROWS, :], right[...], (((1,), (1,)), ((), ())),
            preferred_element_type=jnp.float32,
        )

    counts[...] += hits(0)
    sums0[...] += hits(1) + hits(2) + hits(3)
    sums1[...] += hits(4) + hits(5) + hits(6)


def joined(ref, rows):
    return jnp.concatenate([ref[part, rows, :] for part in range(4)], axis=1)


def gradient_kernel(
    slots, arrived, lap0, base1, base2, counts, sums0, sums1, same_ref, cross_ref,
    outgoing, courant, field1, field2, partial, parts, near, far,
):
    for k in range(APT):
        kx, ky, kz = k // (AY * AZ), (k // AZ) % AY, k % AZ
        tile = arrived[slots[0, k]]
        for part in range(2):
            courant[2 * ky + part, pl.ds(kx * TS * AZ + kz, TS, AZ), :] = tile[:, part * 128 : part * 128 + 128]
    clear_pads(field1)
    clear_pads(field2)
    for x in range(BX):
        rows = slice(x * AZ, x * AZ + AZ)
        speed = joined(courant, rows)
        field1[PAD + x * AZ : PAD + x * AZ + AZ, :] = base1[rows, :] + speed * speed * lap0[rows, :]
    stencil_products(field1, parts, near, far, same_ref, cross_ref)
    upper, keep = far_masks()
    for x in range(BX):
        rows = slice(x * AZ, x * AZ + AZ)
        own = slice(PAD + x * AZ, PAD + x * AZ + AZ)
        speed = joined(courant, rows)
        squared = speed * speed
        bent = laplacian_rows(field1, near, far, x * AZ, upper, keep)
        after = 2.0 * field1[own, :] + base2[rows, :] + squared * bent
        miss2 = counts[rows, :] * after - sums1[rows, :]
        field2[own, :] = squared * miss2
        base = counts[rows, :] * field1[own, :] - sums0[rows, :] + 2.0 * miss2
        partial[rows, :] = miss2 * bent + base * lap0[rows, :]
    stencil_products(field2, parts, near, far, same_ref, cross_ref)
    for x in range(BX):
        rows = slice(x * AZ, x * AZ + AZ)
        bent = laplacian_rows(field2, near, far, x * AZ, upper, keep)
        result = 2.0 * joined(courant, rows) * (partial[rows, :] + bent * lap0[rows, :])
        for part in range(4):
            courant[part, rows, :] = result[:, part * 128 : part * 128 + 128]
    for k in range(APT):
        kx, ky, kz = k // (AY * AZ), (k // AZ) % AY, k % AZ
        for part in range(2):
            outgoing[slots[0, k], :, part * 128 : part * 128 + 128] = courant[
                2 * ky + part, pl.ds(kx * TS * AZ + kz, TS, AZ), :
            ]


def update_kernel(capacity, wanted, returned, velocity, accumulated, new_velocity, new_accumulated, pooled):
    devices = wanted.shape[0]
    block = velocity.shape[0]
    tiles = pooled.shape[0] - 1
    step = pl.program_id(0)

    @pl.when(step == 0)
    def _():
        for tile in range(tiles):
            pooled[tile] = jnp.zeros(pooled.shape[1:], jnp.float32)

        def add(shot, carry):
            for rank in range(capacity):
                tile = wanted[shot, rank]
                tile = jnp.where(tile < 0, tiles, tile)
                pooled[tile] += returned[shot * capacity + rank]
            return carry

        lax.fori_loop(0, devices, add, 0)

    gradient = pooled[pl.ds(step * block, block)]
    total = accumulated[...] + gradient * gradient
    new_accumulated[...] = total
    new_velocity[...] = velocity[...] - step_rate * gradient / jnp.sqrt(total)


VMEM = pl.BlockSpec(memory_space=pltpu.VMEM)
SMEM = pl.BlockSpec(memory_space=pltpu.SMEM)
MIB = 2**20


def params(mib):
    return pltpu.CompilerParams(vmem_limit_bytes=mib * MIB)


def f32(*shape):
    return jax.ShapeDtypeStruct(shape, jnp.float32)


def body(velocity, accumulated, aperture_tiles, source_cell, wavelet, start_field, receiver_cells, observed):
    devices = lax.axis_size("shot")
    per_device = velocity.shape[0]
    capacity = max(2, 2 * APT // devices)
    same, cross = stencil_matrices()
    same = jnp.asarray(same, jnp.bfloat16)
    cross = jnp.asarray(cross, jnp.bfloat16)

    table, slots = pl.pallas_call(
        functools.partial(request_kernel, capacity, per_device),
        out_shape=(
            jax.ShapeDtypeStruct((devices, 128), jnp.int32),
            jax.ShapeDtypeStruct((1, APT), jnp.int32),
        ),
        in_specs=[SMEM],
        out_specs=(VMEM, SMEM),
        scratch_shapes=[pltpu.SMEM((devices,), jnp.int32)],
        name="requests",
    )(aperture_tiles)
    wanted = lax.all_to_all(table, "shot", split_axis=0, concat_axis=0, tiled=True)

    fields = (ROWS, LANES)
    padded = pltpu.VMEM((ROWS + 2 * PAD, LANES), jnp.float32)
    whole = pltpu.VMEM(fields, jnp.float32)
    pieces = pltpu.VMEM((3,) + fields, jnp.bfloat16)
    lap0, base1, base2 = pl.pallas_call(
        prepare_kernel,
        out_shape=(f32(*fields),) * 3,
        in_specs=[SMEM, SMEM, VMEM, VMEM, VMEM],
        out_specs=(VMEM,) * 3,
        scratch_shapes=[padded, pieces, whole, whole],
        compiler_params=params(16),
        cost_estimate=pl.CostEstimate(flops=10**9, bytes_accessed=4 * MIB, transcendentals=0),
        name="prepare",
    )(source_cell, wavelet, start_field[0], same, cross)

    outgoing = pl.pallas_call(
        functools.partial(gather_kernel, capacity),
        out_shape=f32(devices * capacity, *velocity.shape[1:]),
        in_specs=[SMEM, VMEM],
        out_specs=VMEM,
        compiler_params=params(16),
        name="gather",
    )(wanted, velocity)
    arrived = lax.all_to_all(outgoing, "shot", split_axis=0, concat_axis=0, tiled=True)

    receivers = receiver_cells.shape[1]
    counts, sums0, sums1 = pl.pallas_call(
        receivers_kernel,
        out_shape=(f32(*fields),) * 3,
        grid=(receivers // CHUNK,),
        in_specs=[VMEM, VMEM],
        out_specs=(pl.BlockSpec(fields, lambda i: (0, 0)),) * 3,
        scratch_shapes=[
            pltpu.VMEM((7 * ROWS, CHUNK), jnp.bfloat16),
            pltpu.VMEM((LANES, CHUNK), jnp.bfloat16),
        ],
        compiler_params=params(24),
        cost_estimate=pl.CostEstimate(flops=15 * 10**9, bytes_accessed=2 * MIB, transcendentals=0),
        name="receivers",
    )(receiver_cells, observed[0])

    outgoing_gradient = pl.pallas_call(
        gradient_kernel,
        out_shape=f32(devices * capacity, *velocity.shape[1:]),
        in_specs=[SMEM] + [VMEM] * 9,
        out_specs=VMEM,
        scratch_shapes=[pltpu.VMEM((4, ROWS, 128), jnp.float32), padded, padded, whole, pieces, whole, whole],
        compiler_params=params(24),
        name="gradient",
    )(slots, arrived, lap0, base1, base2, counts, sums0, sums1, same, cross)
    returned = lax.all_to_all(outgoing_gradient, "shot", split_axis=0, concat_axis=0, tiled=True)

    tile = velocity.shape[1:]
    block = 8
    by_block = pl.BlockSpec((block,) + tile, lambda i: (i, 0, 0))
    return pl.pallas_call(
        functools.partial(update_kernel, capacity),
        out_shape=(f32(*velocity.shape),) * 2,
        grid=(per_device // block,),
        in_specs=[SMEM, VMEM, by_block, by_block],
        out_specs=(by_block,) * 2,
        scratch_shapes=[pltpu.VMEM((per_device + 1,) + tile, jnp.float32)],
        compiler_params=params(16),
        name="update",
    )(wanted, returned, velocity, accumulated)


def solution(mesh):
    split_shots = ("groups", "shot")
    return jax.shard_map(
        body,
        mesh=mesh,
        in_specs=(
            P(split_shots, None, None),
            P(split_shots, None, None),
            P(split_shots, None),
            P(split_shots),
            P(split_shots, None),
            P(split_shots, None, None, None, None),
            P(split_shots, None),
            P(split_shots, None, None),
        ),
        out_specs=(P(split_shots, None, None), P(split_shots, None, None)),
        check_vma=False,
    )
```

```python
import functools

import jax
import jax.numpy as jnp
import numpy as np
from jax import lax
from jax.experimental import pallas as pl
from jax.experimental.pallas import tpu as pltpu
from jax.sharding import PartitionSpec as P

TS = 16
AX = 2
AY = 2
AZ = 8
BX = AX * TS
BY = AY * TS
APT = AX * AY * AZ
ROWS = BX * AZ
LANES = BY * TS
HALF = TS * TS
PAD = 4 * AZ
CHUNK = 2048
BLOCKS = 8
GROUPS = 4
HELD = 2**16

scaled_weights = (-14350.0, 8064.0, -1008.0, 128.0, -9.0)
weight_scale = 1.0 / 5040.0
step_rate = 0.02


def stencil_matrices():
    lane = np.arange(LANES)
    y, l = lane // TS, lane % TS
    same = np.zeros((LANES, LANES), np.float32)
    cross = np.zeros((LANES, LANES), np.float32)
    for offset in range(1, 5):
        w = scaled_weights[offset]
        dy = np.abs(y[:, None] - y[None, :])
        dl = np.abs(l[:, None] - l[None, :])
        same += w * ((dl == 0) & (dy == offset))
        same += w * ((dy == 0) & (dl == offset))
        cross += w * ((dy == 0) & (dl == TS - offset))
    return same, cross[:HALF, :HALF]


def split(value):
    high = value.astype(jnp.bfloat16)
    rest = value - high.astype(jnp.float32)
    middle = rest.astype(jnp.bfloat16)
    low = (rest - middle.astype(jnp.float32)).astype(jnp.bfloat16)
    return high, middle, low


def joined(ref, row, count):
    rows = slice(row, row + count)
    if len(ref.shape) == 2:
        return ref[rows, :]
    return jnp.concatenate([ref[part, rows, :] for part in range(ref.shape[0])], axis=1)


def stencil_products(field, parts, near, far, same_ref, cross_ref):
    for row in range(0, ROWS, 16):
        pieces = split(joined(field, PAD + row, 16))
        for p in range(3):
            parts[p, row : row + 16, :] = pieces[p]
    same = same_ref[...]
    cross = cross_ref[...]
    dot = functools.partial(jnp.dot, preferred_element_type=jnp.float32)
    near[...] = dot(parts[0], same) + dot(parts[1], same) + dot(parts[2], same)
    for side in range(0, LANES, HALF):
        cols = slice(side, side + HALF)
        far[:, cols] = (
            dot(parts[0, :, cols], cross) + dot(parts[1, :, cols], cross) + dot(parts[2, :, cols], cross)
        )


def laplacian_rows(field, near, far, row, upper, keep):
    at = PAD + row
    total = near[row : row + AZ, :] + 3.0 * scaled_weights[0] * joined(field, at, AZ)
    for offset in range(1, 5):
        pair = joined(field, at + offset * AZ, AZ) + joined(field, at - offset * AZ, AZ)
        total = total + scaled_weights[offset] * pair
    other = far[row : row + AZ, :]
    moved = jnp.where(upper, pltpu.roll(other, AZ - 1, 0), pltpu.roll(other, 1, 0))
    return weight_scale * (total + jnp.where(keep, moved, 0.0))


def far_masks():
    lane = lax.broadcasted_iota(jnp.int32, (AZ, LANES), 1) % TS
    row = lax.broadcasted_iota(jnp.int32, (AZ, LANES), 0)
    upper = lane >= TS // 2
    keep = row != jnp.where(upper, AZ - 1, 0)
    return upper, keep


def clear_pads(field):
    zero = jnp.zeros(field.shape[:-2] + (PAD, field.shape[-1]), jnp.float32)
    field[..., :PAD, :] = zero
    field[..., PAD + ROWS :, :] = zero


def slot_of(capacity, per_device, ids, k, counts):
    tile = ids[0, k]
    owner = tile // per_device
    rank = counts[owner]
    counts[owner] = rank + 1
    return owner * capacity + rank, tile - owner * per_device


def request_kernel(capacity, per_device, ids, table, counts):
    devices = table.shape[0]
    for owner in range(devices):
        counts[owner] = 0
    owner_of = lax.broadcasted_iota(jnp.int32, table.shape, 0)
    rank_of = lax.broadcasted_iota(jnp.int32, table.shape, 1)
    position = owner_of * capacity + jnp.where(rank_of < capacity, rank_of, -devices * capacity)
    found = jnp.full(table.shape, -1, jnp.int32)
    for k in range(APT):
        slot, tile = slot_of(capacity, per_device, ids, k, counts)
        found = jnp.where(position == slot, tile, found)
    table[...] = found


def gather_kernel(capacity, wanted_in, velocity, outgoing, wanted, owned, held, fetched, sent):
    devices = wanted_in.shape[0]
    listed = pltpu.make_async_copy(wanted_in, wanted, fetched.at[GROUPS])
    listed.start()
    tiles = velocity.shape[0] // GROUPS
    copies = [
        pltpu.make_async_copy(
            velocity.at[g * tiles : (g + 1) * tiles], owned.at[g * tiles : (g + 1) * tiles], fetched.at[g]
        )
        for g in range(GROUPS)
    ]
    for copy in copies:
        copy.start()
    listed.wait()
    for copy in copies:
        copy.wait()
    shots = devices // GROUPS
    copies = []
    for g in range(GROUPS):

        def step(shot, carry):
            for rank in range(capacity):
                held[shot * capacity + rank] = owned[jnp.maximum(wanted[shot, rank], 0)]
            return carry

        lax.fori_loop(g * shots, (g + 1) * shots, step, 0, unroll=True)
        part = slice(g * shots * capacity, (g + 1) * shots * capacity)
        copies.append(pltpu.make_async_copy(held.at[part], outgoing.at[part], sent.at[g]))
        copies[-1].start()
    for copy in copies:
        copy.wait()


def turn(start, step, x, y):
    group = lax.broadcasted_iota(jnp.int32, (8, 128), 1) // TS
    held = [start[step, pl.ds(x * BY + y + j, 8, BY), :] for j in range(8)]
    for bit in (1, 2, 4):
        low = (group & bit) == 0
        for j in range(8):
            if j & bit == 0:
                one, two = held[j], held[j + bit]
                held[j] = jnp.where(low, one, pltpu.roll(two, bit * TS, 1))
                held[j + bit] = jnp.where(low, pltpu.roll(one, 128 - bit * TS, 1), two)
    return held


def prepare(source, wavelet, start, same_ref, cross_ref, lap0, base1, base2, current, previous, parts, near, far):
    clear_pads(current)
    cell = source[0]
    sx, sy, sz = cell // (BY * AZ * TS), (cell // (AZ * TS)) % BY, cell % (AZ * TS)
    source_row = sx * AZ + sz // TS
    source_lane = sy * TS + sz % TS
    place = lax.broadcasted_iota(jnp.int32, (AZ, LANES), 0) * LANES + lax.broadcasted_iota(jnp.int32, (AZ, LANES), 1)

    for x in range(0, BX, 8):
        for y in range(0, BY, 8):
            old = turn(start, 0, x, y)
            new = turn(start, 1, x, y)
            for kz in range(AZ):
                previous[y // 8, pl.ds(x * AZ + kz, 8, AZ), :] = old[kz]
                current[y // 8, pl.ds(PAD + x * AZ + kz, 8, AZ), :] = new[kz]
    for x in range(BX):
        hit = place == (source_row - x * AZ) * LANES + source_lane
        rows = slice(x * AZ, x * AZ + AZ)
        now = joined(current, PAD + x * AZ, AZ)
        base1[rows, :] = 2.0 * now - joined(previous, x * AZ, AZ) + jnp.where(hit, wavelet[0, 0], 0.0)
        base2[rows, :] = jnp.where(hit, wavelet[0, 1], 0.0) - now
    stencil_products(current, parts, near, far, same_ref, cross_ref)
    upper, keep = far_masks()
    for x in range(BX):
        lap0[x * AZ : x * AZ + AZ, :] = laplacian_rows(current, near, far, x * AZ, upper, keep)


def local_kernel(
    capacity, per_device, cells, recorded, ids, source, wavelet, start, same_ref, cross_ref,
    fields_out, slots_out, same_out, cross_out,
    lap0, base1, base2, current, previous, parts, near, far, left, right, total, slots, counts, done,
):
    step = pl.program_id(0)
    last = pl.num_programs(0) - 1
    outputs = [
        (lap0, fields_out.at[:ROWS]),
        (base1, fields_out.at[ROWS : 2 * ROWS]),
        (base2, fields_out.at[2 * ROWS : 3 * ROWS]),
        (slots, slots_out.at[:1]),
        (same_ref, same_out.at[:LANES]),
        (cross_ref, cross_out.at[:HALF]),
    ]
    outputs = [pltpu.make_async_copy(a, b, done.at[n]) for n, (a, b) in enumerate(outputs)]

    @pl.when(step == 0)
    def _():
        total[...] = jnp.zeros_like(total)
        for owner in range(counts.shape[0]):
            counts[owner] = 0
        for k in range(APT):
            slots[0, k], _ = slot_of(capacity, per_device, ids, k, counts)
        prepare(source, wavelet, start, same_ref, cross_ref, lap0, base1, base2, current, previous, parts, near, far)
        for copy in outputs:
            copy.start()

    @pl.when(step < last)
    def _():
        here = pl.ds(pl.multiple_of(step * CHUNK, CHUNK), CHUNK)
        cell = cells[:, here]
        x, y, z = cell // (BY * AZ * TS), (cell // (AZ * TS)) % BY, cell % (AZ * TS)
        row = x * AZ + z // TS
        lane = y * TS + z % TS
        for at in range(0, LANES, 16):
            ids = lax.broadcasted_iota(jnp.int32, (16, CHUNK), 0) + at
            right[at : at + 16, :] = jnp.where(ids == lane, 1.0, 0.0).astype(jnp.bfloat16)
        pieces = []
        for n in range(2):
            pieces += split(jnp.broadcast_to(recorded[n : n + 1, here], (16, CHUNK)))
        for at in range(0, ROWS, 16):
            ids = lax.broadcasted_iota(jnp.int32, (16, CHUNK), 0) + at
            hot = jnp.where(ids == row, 1.0, 0.0).astype(jnp.bfloat16)
            left[at : at + 16, :] = hot
            for p in range(6):
                left[(p + 1) * ROWS + at : (p + 1) * ROWS + at + 16, :] = hot * pieces[p]
        total[...] += lax.dot_general(
            left[...], right[...], (((1,), (1,)), ((), ())), preferred_element_type=jnp.float32
        )

    @pl.when(step == last)
    def _():
        def part(n):
            return total[n * ROWS : (n + 1) * ROWS, :]

        total[ROWS : 2 * ROWS, :] = part(1) + part(2) + part(3)
        total[2 * ROWS : 3 * ROWS, :] = part(4) + part(5) + part(6)
        copy = pltpu.make_async_copy(total.at[: 3 * ROWS], fields_out.at[3 * ROWS : 6 * ROWS], done.at[6])
        copy.start()
        copy.wait()
        for copy in outputs:
            copy.wait()


def gradient_kernel(
    arrived, fields_in, slots_in, same_in, cross_in, outgoing,
    slots, same_ref, cross_ref, lap0, base1, base2, counts, sums0, sums1,
    courant, field1, field2, partial, parts, near, far, done,
):
    inputs = [(slots_in.at[:1], slots)]
    inputs += [
        (fields_in.at[n * ROWS : (n + 1) * ROWS], target)
        for n, target in enumerate((lap0, base1, base2, counts, sums0, sums1))
    ]
    inputs += [(same_in.at[:LANES], same_ref), (cross_in.at[:HALF], cross_ref)]
    copies = [pltpu.make_async_copy(a, b, done.at[n]) for n, (a, b) in enumerate(inputs)]
    for n in (0, 1, 2, 7, 8, 3, 4, 5, 6):
        copies[n].start()
    clear_pads(field1)
    clear_pads(field2)
    copies[0].wait()
    for k in range(APT):
        kx, ky, kz = k // (AY * AZ), (k // AZ) % AY, k % AZ
        tile = arrived[slots[0, k]]
        for part in range(2):
            courant[2 * ky + part, pl.ds(kx * TS * AZ + kz, TS, AZ), :] = tile[:, part * 128 : part * 128 + 128]
    copies[1].wait()
    copies[2].wait()
    for x in range(BX):
        rows = slice(x * AZ, x * AZ + AZ)
        speed = joined(courant, x * AZ, AZ)
        field1[PAD + x * AZ : PAD + x * AZ + AZ, :] = base1[rows, :] + speed * speed * lap0[rows, :]
    copies[7].wait()
    copies[8].wait()
    stencil_products(field1, parts, near, far, same_ref, cross_ref)
    upper, keep = far_masks()
    for copy in copies[3:7]:
        copy.wait()
    for x in range(BX):
        rows = slice(x * AZ, x * AZ + AZ)
        own = slice(PAD + x * AZ, PAD + x * AZ + AZ)
        speed = joined(courant, x * AZ, AZ)
        squared = speed * speed
        bent = laplacian_rows(field1, near, far, x * AZ, upper, keep)
        after = 2.0 * field1[own, :] + base2[rows, :] + squared * bent
        miss2 = counts[rows, :] * after - sums1[rows, :]
        field2[own, :] = squared * miss2
        base = counts[rows, :] * field1[own, :] - sums0[rows, :] + 2.0 * miss2
        partial[rows, :] = miss2 * bent + base * lap0[rows, :]
    stencil_products(field2, parts, near, far, same_ref, cross_ref)
    for x in range(BX):
        rows = slice(x * AZ, x * AZ + AZ)
        bent = laplacian_rows(field2, near, far, x * AZ, upper, keep)
        result = 2.0 * joined(courant, x * AZ, AZ) * (partial[rows, :] + bent * lap0[rows, :])
        for part in range(4):
            courant[part, rows, :] = result[:, part * 128 : part * 128 + 128]
    for k in range(APT):
        kx, ky, kz = k // (AY * AZ), (k // AZ) % AY, k % AZ
        for part in range(2):
            outgoing[slots[0, k], :, part * 128 : part * 128 + 128] = courant[
                2 * ky + part, pl.ds(kx * TS * AZ + kz, TS, AZ), :
            ]


def update_kernel(
    capacity, wanted, returned, velocity, accumulated, velocity_out, accumulated_out,
    pooled, new_velocity, new_accumulated, done,
):
    devices = wanted.shape[0]
    tiles = velocity.shape[0]
    zero = jnp.zeros(pooled.shape[1:], jnp.float32)
    for tile in range(tiles):
        pooled[tile] = zero

    def add(shot, carry):
        for rank in range(capacity):
            tile = wanted[shot, rank]
            tile = jnp.where(tile < 0, tiles, tile)
            pooled[tile] += returned[shot * capacity + rank]
        return carry

    lax.fori_loop(0, devices, add, 0, unroll=2)
    block = tiles // BLOCKS
    copies = []
    for n in range(BLOCKS):
        here = slice(n * block, (n + 1) * block)
        gradient = pooled[here]
        total = accumulated[here] + gradient * gradient
        new_accumulated[here] = total
        new_velocity[here] = velocity[here] - step_rate * gradient / jnp.sqrt(total)
        for which, (source, target) in enumerate(((new_velocity, velocity_out), (new_accumulated, accumulated_out))):
            copies.append(pltpu.make_async_copy(source.at[here], target.at[here], done.at[which, n]))
            copies[-1].start()
    for copy in copies:
        copy.wait()


VMEM = pl.BlockSpec(memory_space=pltpu.VMEM)
HBM = pl.BlockSpec(memory_space=pltpu.HBM)
SMEM = pl.BlockSpec(memory_space=pltpu.SMEM)
MIB = 2**20


def params(mib):
    return pltpu.CompilerParams(vmem_limit_bytes=mib * MIB)


def f32(*shape):
    return jax.ShapeDtypeStruct(shape, jnp.float32)


def body(velocity, accumulated, aperture_tiles, source_cell, wavelet, start_field, receiver_cells, observed):
    devices = lax.axis_size("shot")
    per_device = velocity.shape[0]
    capacity = max(2, 2 * APT // devices)
    same, cross = stencil_matrices()
    same = jnp.asarray(same, jnp.bfloat16)
    cross = jnp.asarray(cross, jnp.bfloat16)

    table = pl.pallas_call(
        functools.partial(request_kernel, capacity, per_device),
        out_shape=jax.ShapeDtypeStruct((devices, 128), jnp.int32),
        in_specs=[SMEM],
        out_specs=VMEM,
        scratch_shapes=[pltpu.SMEM((devices,), jnp.int32)],
        name="requests",
    )(aperture_tiles)
    wanted = lax.all_to_all(table, "shot", split_axis=0, concat_axis=0, tiled=True)

    fields = (ROWS, LANES)
    padded = pltpu.VMEM((ROWS + 2 * PAD, LANES), jnp.float32)
    whole = pltpu.VMEM(fields, jnp.float32)
    quarters = pltpu.VMEM((LANES // 128, ROWS, 128), jnp.float32)
    padded_quarters = pltpu.VMEM((LANES // 128, ROWS + 2 * PAD, 128), jnp.float32)
    pieces = pltpu.VMEM((3,) + fields, jnp.bfloat16)
    dma = pltpu.SemaphoreType.DMA
    slots_total = devices * capacity
    held = pltpu.VMEM((slots_total,) + velocity.shape[1:], jnp.float32)
    owned = pltpu.VMEM(velocity.shape, jnp.float32)
    outgoing = pl.pallas_call(
        functools.partial(gather_kernel, capacity),
        out_shape=f32(slots_total, *velocity.shape[1:]),
        in_specs=[HBM, HBM],
        out_specs=HBM,
        scratch_shapes=[pltpu.SMEM(wanted.shape, jnp.int32), owned, held, dma((GROUPS + 1,)), dma((GROUPS,))],
        compiler_params=params(62),
        name="gather",
    )(wanted, velocity)
    arrived = lax.all_to_all(outgoing, "shot", split_axis=0, concat_axis=0, tiled=True)

    receivers = receiver_cells.shape[1]
    list_memory = pltpu.SMEM((1, 128), jnp.int32)
    held_bytes = HELD * 128 * 4
    constants = [pltpu.VMEM(same.shape, same.dtype), pltpu.VMEM(cross.shape, cross.dtype)]
    fields_held, slots_held, same_held, cross_held = pl.pallas_call(
        functools.partial(local_kernel, capacity, per_device),
        out_shape=(
            f32(held_bytes // (4 * LANES), LANES),
            jax.ShapeDtypeStruct((held_bytes // (4 * 128), 128), jnp.int32),
            jax.ShapeDtypeStruct((held_bytes // (2 * LANES), LANES), jnp.bfloat16),
            jax.ShapeDtypeStruct((held_bytes // (2 * HALF), HALF), jnp.bfloat16),
        ),
        grid=(receivers // CHUNK + 1,),
        in_specs=[VMEM, VMEM, SMEM, SMEM, SMEM, VMEM, VMEM, VMEM],
        out_specs=(HBM,) * 4,
        scratch_shapes=[
            whole, whole, whole, padded_quarters, quarters, pieces, whole, whole,
            pltpu.VMEM((7 * ROWS, CHUNK), jnp.bfloat16),
            pltpu.VMEM((LANES, CHUNK), jnp.bfloat16),
            pltpu.VMEM((7 * ROWS, LANES), jnp.float32),
            list_memory,
            pltpu.SMEM((devices,), jnp.int32),
            dma((7,)),
        ],
        compiler_params=params(62),
        cost_estimate=pl.CostEstimate(flops=16 * 10**9, bytes_accessed=4 * MIB, transcendentals=0),
        name="local",
    )(
        receiver_cells, observed[0], aperture_tiles, source_cell, wavelet,
        start_field.reshape(2, BX * BY, AZ * TS), same, cross,
    )

    outgoing_gradient = pl.pallas_call(
        gradient_kernel,
        out_shape=f32(slots_total, *velocity.shape[1:]),
        in_specs=[VMEM, HBM, HBM, HBM, HBM],
        out_specs=VMEM,
        scratch_shapes=[
            list_memory, *constants, whole, whole, whole, whole, whole, whole,
            quarters, padded, padded, whole, pieces, whole, whole, dma((9,)),
        ],
        compiler_params=params(40),
        name="gradient",
    )(arrived, fields_held, slots_held, same_held, cross_held)
    returned = lax.all_to_all(outgoing_gradient, "shot", split_axis=0, concat_axis=0, tiled=True)

    tile = velocity.shape[1:]
    return pl.pallas_call(
        functools.partial(update_kernel, capacity),
        out_shape=(f32(*velocity.shape),) * 2,
        in_specs=[SMEM, VMEM, VMEM, VMEM],
        out_specs=(HBM,) * 2,
        scratch_shapes=[pltpu.VMEM((per_device + 1,) + tile, jnp.float32), owned, owned, dma((2, BLOCKS))],
        compiler_params=params(16),
        name="update",
    )(wanted, returned, velocity, accumulated)


def solution(mesh):
    split_shots = ("groups", "shot")
    return jax.shard_map(
        body,
        mesh=mesh,
        in_specs=(
            P(split_shots, None, None),
            P(split_shots, None, None),
            P(split_shots, None),
            P(split_shots),
            P(split_shots, None),
            P(split_shots, None, None, None, None),
            P(split_shots, None),
            P(split_shots, None, None),
        ),
        out_specs=(P(split_shots, None, None), P(split_shots, None, None)),
        check_vma=False,
    )
```

```python
import functools

import jax
import jax.numpy as jnp
import numpy as np
from jax import lax
from jax.experimental import pallas as pl
from jax.experimental.pallas import tpu as pltpu
from jax.sharding import PartitionSpec as P

TS = 16
AX = 2
AY = 2
AZ = 8
BX = AX * TS
BY = AY * TS
APT = AX * AY * AZ
ROWS = BX * AZ
LANES = BY * TS
HALF = TS * TS
BLOCKS = 8
GROUPS = 4
HELD = 2**16

scaled_weights = (-14350.0, 8064.0, -1008.0, 128.0, -9.0)
weight_scale = 1.0 / 5040.0
step_rate = 0.02


def stencil_matrices():
    lane = np.arange(LANES)
    y, l = lane // TS, lane % TS
    same = np.zeros((LANES, LANES), np.float32)
    cross = np.zeros((LANES, LANES), np.float32)
    for offset in range(1, 5):
        w = scaled_weights[offset]
        dy = np.abs(y[:, None] - y[None, :])
        dl = np.abs(l[:, None] - l[None, :])
        same += w * ((dl == 0) & (dy == offset))
        same += w * ((dy == 0) & (dl == offset))
        cross += w * ((dy == 0) & (dl == TS - offset))
    row = np.arange(ROWS)
    x, kz = row // (AZ * TS) * TS + row % TS, row // TS % AZ
    down = np.zeros((ROWS, ROWS), np.float32)
    for offset in range(1, 5):
        distance = np.abs(x[:, None] - x[None, :])
        down += scaled_weights[offset] * ((kz[:, None] == kz[None, :]) & (distance == offset))
    return same, np.concatenate([cross[:HALF, :HALF], down], axis=0)


def split(value):
    high = value.astype(jnp.bfloat16)
    rest = value - high.astype(jnp.float32)
    middle = rest.astype(jnp.bfloat16)
    low = (rest - middle.astype(jnp.float32)).astype(jnp.bfloat16)
    return high, middle, low


def stencil_products(field, parts, near, far, same_ref, cross_ref):
    for row in range(0, ROWS, 16):
        pieces = split(field[row : row + 16, :])
        for p in range(3):
            parts[p, row : row + 16, :] = pieces[p]
    same = same_ref[...]
    cross = cross_ref[:HALF, :]
    down = cross_ref[HALF:, :]
    dot = functools.partial(jnp.dot, preferred_element_type=jnp.float32)
    near[...] = dot(parts[0], same) + dot(parts[1], same) + dot(parts[2], same)
    near[...] += dot(down, parts[0]) + dot(down, parts[1]) + dot(down, parts[2])
    for side in range(0, LANES, HALF):
        cols = slice(side, side + HALF)
        far[:, cols] = (
            dot(parts[0, :, cols], cross) + dot(parts[1, :, cols], cross) + dot(parts[2, :, cols], cross)
        )


def laplacian_rows(field, near, far, row, upper):
    total = near[row : row + 8, :] + 3.0 * scaled_weights[0] * field[row : row + 8, :]
    kz = row // TS % AZ
    zero = jnp.zeros((8, LANES), jnp.float32)
    after = far[row + TS : row + TS + 8, :] if kz < AZ - 1 else zero
    before = far[row - TS : row - TS + 8, :] if kz > 0 else zero
    return weight_scale * (total + jnp.where(upper, after, before))


def upper_half():
    return lax.broadcasted_iota(jnp.int32, (8, LANES), 1) % TS >= TS // 2


def tile_row(x, z):
    return (x // TS * AZ + z // TS) * TS + x % TS


def slot_of(capacity, per_device, ids, k, counts):
    tile = ids[0, k]
    owner = tile // per_device
    rank = counts[owner]
    counts[owner] = rank + 1
    return owner * capacity + rank, tile - owner * per_device


def request_kernel(capacity, per_device, ids, table, counts):
    devices = table.shape[0]
    for owner in range(devices):
        counts[owner] = 0
    owner_of = lax.broadcasted_iota(jnp.int32, table.shape, 0)
    rank_of = lax.broadcasted_iota(jnp.int32, table.shape, 1)
    position = owner_of * capacity + jnp.where(rank_of < capacity, rank_of, -devices * capacity)
    found = jnp.full(table.shape, -1, jnp.int32)
    for k in range(APT):
        slot, tile = slot_of(capacity, per_device, ids, k, counts)
        found = jnp.where(position == slot, tile, found)
    table[...] = found


def gather_kernel(capacity, wanted_in, velocity, outgoing, wanted, owned, held, fetched, sent):
    devices = wanted_in.shape[0]
    listed = pltpu.make_async_copy(wanted_in, wanted, fetched.at[GROUPS])
    listed.start()
    tiles = velocity.shape[0] // GROUPS
    copies = [
        pltpu.make_async_copy(
            velocity.at[g * tiles : (g + 1) * tiles], owned.at[g * tiles : (g + 1) * tiles], fetched.at[g]
        )
        for g in range(GROUPS)
    ]
    for copy in copies:
        copy.start()
    listed.wait()
    for copy in copies:
        copy.wait()
    shots = devices // GROUPS
    copies = []
    for g in range(GROUPS):

        def step(shot, carry):
            for rank in range(capacity):
                held[shot * capacity + rank] = owned[jnp.maximum(wanted[shot, rank], 0)]
            return carry

        lax.fori_loop(g * shots, (g + 1) * shots, step, 0, unroll=True)
        part = slice(g * shots * capacity, (g + 1) * shots * capacity)
        copies.append(pltpu.make_async_copy(held.at[part], outgoing.at[part], sent.at[g]))
        copies[-1].start()
    for copy in copies:
        copy.wait()


def turn(start, step, x, y):
    group = lax.broadcasted_iota(jnp.int32, (8, 128), 1) // TS
    held = [start[step, pl.ds(x * BY + y + j, 8, BY), :] for j in range(8)]
    for bit in (1, 2, 4):
        low = (group & bit) == 0
        for j in range(8):
            if j & bit == 0:
                one, two = held[j], held[j + bit]
                held[j] = jnp.where(low, one, pltpu.roll(two, bit * TS, 1))
                held[j + bit] = jnp.where(low, pltpu.roll(one, 128 - bit * TS, 1), two)
    return held


def local_kernel(
    capacity, per_device, cells, recorded, ids, source, wavelet, start_in, same_ref, cross_ref,
    fields_out, slots_out, same_out, cross_out,
    start, lap0, base1, base2, current, parts, near, far, left, right, total, slots, counts, done,
):
    step = pl.program_id(0)
    last = pl.num_programs(0) - 1
    chunk = left.shape[1]

    def copy_of(n, held, target):
        return pltpu.make_async_copy(held, target, done.at[n])

    lists = [
        copy_of(0, slots, slots_out.at[:1]),
        copy_of(1, same_ref, same_out.at[:LANES]),
        copy_of(2, cross_ref, cross_out.at[: HALF + ROWS]),
    ]
    bases = [copy_of(3, base1, fields_out.at[ROWS : 2 * ROWS])]
    results = [
        copy_of(4, total.at[: 3 * ROWS], fields_out.at[2 * ROWS : 5 * ROWS]),
        copy_of(5, lap0, fields_out.at[:ROWS]),
    ]

    @pl.when(step == 0)
    def _():
        copies = [copy_of(6 + n, start_in.at[n], start.at[n, : BX * BY]) for n in range(2)]
        for copy in copies:
            copy.start()
        total[...] = jnp.zeros_like(total)
        for owner in range(counts.shape[0]):
            counts[owner] = 0
        for k in range(APT):
            slots[0, k], _ = slot_of(capacity, per_device, ids, k, counts)
        for copy in lists:
            copy.start()
        for copy in copies:
            copy.wait()

    @pl.when(step < last)
    def _():
        here = pl.ds(pl.multiple_of(step * chunk, chunk), chunk)
        cell = cells[:, here]
        x, y, z = cell // (BY * AZ * TS), (cell // (AZ * TS)) % BY, cell % (AZ * TS)
        row = tile_row(x, z)
        lane = y * TS + z % TS
        for at in range(0, LANES, 16):
            numbers = lax.broadcasted_iota(jnp.int32, (16, chunk), 0) + at
            right[at : at + 16, :] = jnp.where(numbers == lane, 1.0, 0.0).astype(jnp.bfloat16)
        pieces = []
        for n in range(2):
            pieces += split(jnp.broadcast_to(recorded[n : n + 1, here], (16, chunk)))
        for at in range(0, ROWS, 16):
            numbers = lax.broadcasted_iota(jnp.int32, (16, chunk), 0) + at
            hot = jnp.where(numbers == row, 1.0, 0.0).astype(jnp.bfloat16)
            left[at : at + 16, :] = hot
            for p in range(6):
                left[(p + 1) * ROWS + at : (p + 1) * ROWS + at + 16, :] = hot * pieces[p]
        total[...] += lax.dot_general(
            left[...], right[...], (((1,), (1,)), ((), ())), preferred_element_type=jnp.float32
        )

        cell = source[0]
        sx, sy, sz = cell // (BY * AZ * TS), (cell // (AZ * TS)) % BY, cell % (AZ * TS)
        source_row = tile_row(sx, sz)
        source_lane = sy * TS + sz % TS
        place = lax.broadcasted_iota(jnp.int32, (8, LANES), 0) * LANES + lax.broadcasted_iota(
            jnp.int32, (8, LANES), 1
        )
        first = step * 8
        old = [turn(start, 0, first, y) for y in range(0, BY, 8)]
        new = [turn(start, 1, first, y) for y in range(0, BY, 8)]
        for kz in range(AZ):
            at = pl.multiple_of((first // TS * AZ + kz) * TS + first % TS, 8)
            hit = place == (source_row - at) * LANES + source_lane
            rows = pl.ds(at, 8)
            now = jnp.concatenate([part[kz] for part in new], axis=1)
            before = jnp.concatenate([part[kz] for part in old], axis=1)
            current[rows, :] = now
            base1[rows, :] = 2.0 * now - before + jnp.where(hit, wavelet[0, 0], 0.0)
            base2[rows, :] = jnp.where(hit, wavelet[0, 1], 0.0) - now

    @pl.when(step == last)
    def _():
        for copy in bases:
            copy.start()

        def part(n):
            return total[n * ROWS : (n + 1) * ROWS, :]

        total[ROWS : 2 * ROWS, :] = part(1) + part(2) + part(3)
        total[2 * ROWS : 3 * ROWS, :] = part(0) * base2[...] - (part(4) + part(5) + part(6))
        results[0].start()
        stencil_products(current, parts, near, far, same_ref, cross_ref)
        upper = upper_half()
        for row in range(0, ROWS, 8):
            lap0[row : row + 8, :] = laplacian_rows(current, near, far, row, upper)
        results[1].start()
        for copy in lists + bases + results:
            copy.wait()


def gradient_kernel(
    arrived, fields_in, slots_in, same_in, cross_in, outgoing,
    slots, same_ref, cross_ref, lap0, base1, counts, sums0, known1,
    courant, field1, field2, partial, parts, near, far, done,
):
    inputs = [(slots_in.at[:1], slots)]
    inputs += [
        (fields_in.at[n * ROWS : (n + 1) * ROWS], target)
        for n, target in enumerate((lap0, base1, counts, sums0, known1))
    ]
    inputs += [(same_in.at[:LANES], same_ref), (cross_in.at[: HALF + ROWS], cross_ref)]
    copies = [pltpu.make_async_copy(a, b, done.at[n]) for n, (a, b) in enumerate(inputs)]
    for n in (0, 1, 2, 6, 7, 3, 5, 4):
        copies[n].start()
    copies[0].wait()
    copies[1].wait()
    copies[2].wait()
    for k in range(APT):
        kx, ky, kz = k // (AY * AZ), (k // AZ) % AY, k % AZ
        rows = slice((kx * AZ + kz) * TS, (kx * AZ + kz + 1) * TS)
        cols = slice(ky * HALF, (ky + 1) * HALF)
        speed = arrived[slots[0, k]]
        courant[rows, cols] = speed
        field1[rows, cols] = base1[rows, cols] + speed * speed * lap0[rows, cols]
    copies[6].wait()
    copies[7].wait()
    stencil_products(field1, parts, near, far, same_ref, cross_ref)
    upper = upper_half()
    for copy in copies[3:6]:
        copy.wait()
    for row in range(0, ROWS, 8):
        rows = slice(row, row + 8)
        speed = courant[rows, :]
        squared = speed * speed
        bent = laplacian_rows(field1, near, far, row, upper)
        miss2 = counts[rows, :] * (2.0 * field1[rows, :] + squared * bent) + known1[rows, :]
        field2[rows, :] = squared * miss2
        base = counts[rows, :] * field1[rows, :] - sums0[rows, :] + 2.0 * miss2
        partial[rows, :] = miss2 * bent + base * lap0[rows, :]
    stencil_products(field2, parts, near, far, same_ref, cross_ref)
    for kx in range(AX):
        for kz in range(AZ):
            for half in range(0, TS, 8):
                row = (kx * AZ + kz) * TS + half
                rows = slice(row, row + 8)
                bent = laplacian_rows(field2, near, far, row, upper)
                result = 2.0 * courant[rows, :] * (partial[rows, :] + bent * lap0[rows, :])
                for ky in range(AY):
                    slot = slots[0, (kx * AY + ky) * AZ + kz]
                    outgoing[slot, half : half + 8, :] = result[:, ky * HALF : (ky + 1) * HALF]


def update_kernel(
    capacity, wanted_in, returned, velocity, accumulated, velocity_out, accumulated_out,
    wanted, pooled, new_velocity, new_accumulated, listed, done,
):
    devices = wanted.shape[0]
    tiles = velocity.shape[0]
    copy = pltpu.make_async_copy(wanted_in, wanted, listed)
    copy.start()
    zero = jnp.zeros(pooled.shape[1:], jnp.float32)
    for tile in range(tiles):
        pooled[tile] = zero
    copy.wait()

    def add(shot, carry):
        for rank in range(capacity):
            tile = wanted[shot, rank]
            tile = jnp.where(tile < 0, tiles, tile)
            pooled[tile] += returned[shot * capacity + rank]
        return carry

    lax.fori_loop(0, devices, add, 0, unroll=8)
    block = tiles // BLOCKS
    copies = []
    for n in range(BLOCKS):
        here = slice(n * block, (n + 1) * block)
        gradient = pooled[here]
        total = accumulated[here] + gradient * gradient
        new_accumulated[here] = total
        new_velocity[here] = velocity[here] - step_rate * gradient * lax.rsqrt(total)
        for which, (source, target) in enumerate(((new_velocity, velocity_out), (new_accumulated, accumulated_out))):
            copies.append(pltpu.make_async_copy(source.at[here], target.at[here], done.at[which, n]))
            copies[-1].start()
    for copy in copies:
        copy.wait()


VMEM = pl.BlockSpec(memory_space=pltpu.VMEM)
HBM = pl.BlockSpec(memory_space=pltpu.HBM)
SMEM = pl.BlockSpec(memory_space=pltpu.SMEM)
MIB = 2**20


def params(mib):
    return pltpu.CompilerParams(vmem_limit_bytes=mib * MIB)


def f32(*shape):
    return jax.ShapeDtypeStruct(shape, jnp.float32)


def body(velocity, accumulated, aperture_tiles, source_cell, wavelet, start_field, receiver_cells, observed):
    devices = lax.axis_size("shot")
    per_device = velocity.shape[0]
    capacity = max(2, 2 * APT // devices)
    same, cross = stencil_matrices()
    same = jnp.asarray(same, jnp.bfloat16)
    cross = jnp.asarray(cross, jnp.bfloat16)

    table = pl.pallas_call(
        functools.partial(request_kernel, capacity, per_device),
        out_shape=jax.ShapeDtypeStruct((devices, 128), jnp.int32),
        in_specs=[SMEM],
        out_specs=VMEM,
        scratch_shapes=[pltpu.SMEM((devices,), jnp.int32)],
        name="requests",
    )(aperture_tiles)
    wanted = lax.all_to_all(table, "shot", split_axis=0, concat_axis=0, tiled=True)

    fields = (ROWS, LANES)
    whole = pltpu.VMEM(fields, jnp.float32)
    pieces = pltpu.VMEM((3,) + fields, jnp.bfloat16)
    dma = pltpu.SemaphoreType.DMA
    slots_total = devices * capacity
    held = pltpu.VMEM((slots_total,) + velocity.shape[1:], jnp.float32)
    owned = pltpu.VMEM(velocity.shape, jnp.float32)
    outgoing = pl.pallas_call(
        functools.partial(gather_kernel, capacity),
        out_shape=f32(slots_total, *velocity.shape[1:]),
        in_specs=[HBM, HBM],
        out_specs=HBM,
        scratch_shapes=[pltpu.SMEM(wanted.shape, jnp.int32), owned, held, dma((GROUPS + 1,)), dma((GROUPS,))],
        compiler_params=params(62),
        name="gather",
    )(wanted, velocity)
    arrived = lax.all_to_all(outgoing, "shot", split_axis=0, concat_axis=0, tiled=True)

    chunk = receiver_cells.shape[1] // (BX // 8)
    list_memory = pltpu.SMEM((1, 128), jnp.int32)
    held_bytes = HELD * 128 * 4
    constants = [pltpu.VMEM(same.shape, same.dtype), pltpu.VMEM(cross.shape, cross.dtype)]
    fields_held, slots_held, same_held, cross_held = pl.pallas_call(
        functools.partial(local_kernel, capacity, per_device),
        out_shape=(
            f32(held_bytes // (4 * LANES), LANES),
            jax.ShapeDtypeStruct((held_bytes // (4 * 128), 128), jnp.int32),
            jax.ShapeDtypeStruct((held_bytes // (2 * LANES), LANES), jnp.bfloat16),
            jax.ShapeDtypeStruct((held_bytes // (2 * HALF), HALF), jnp.bfloat16),
        ),
        grid=(BX // 8 + 1,),
        in_specs=[VMEM, VMEM, SMEM, SMEM, SMEM, HBM, VMEM, VMEM],
        out_specs=(HBM,) * 4,
        scratch_shapes=[
            pltpu.VMEM((2, BX * BY + 8 * BY, AZ * TS), jnp.float32),
            whole, whole, whole, whole, pieces, whole, whole,
            pltpu.VMEM((7 * ROWS, chunk), jnp.bfloat16),
            pltpu.VMEM((LANES, chunk), jnp.bfloat16),
            pltpu.VMEM((7 * ROWS, LANES), jnp.float32),
            list_memory,
            pltpu.SMEM((devices,), jnp.int32),
            dma((8,)),
        ],
        compiler_params=params(62),
        cost_estimate=pl.CostEstimate(flops=16 * 10**9, bytes_accessed=4 * MIB, transcendentals=0),
        name="local",
    )(
        receiver_cells, observed[0], aperture_tiles, source_cell, wavelet,
        start_field.reshape(2, BX * BY, AZ * TS), same, cross,
    )

    outgoing_gradient = pl.pallas_call(
        gradient_kernel,
        out_shape=f32(slots_total, *velocity.shape[1:]),
        in_specs=[VMEM, HBM, HBM, HBM, HBM],
        out_specs=VMEM,
        scratch_shapes=[
            list_memory, *constants, whole, whole, whole, whole, whole,
            whole, whole, whole, whole, pieces, whole, whole, dma((8,)),
        ],
        compiler_params=params(40),
        name="gradient",
    )(arrived, fields_held, slots_held, same_held, cross_held)
    returned = lax.all_to_all(outgoing_gradient, "shot", split_axis=0, concat_axis=0, tiled=True)

    tile = velocity.shape[1:]
    return pl.pallas_call(
        functools.partial(update_kernel, capacity),
        out_shape=(f32(*velocity.shape),) * 2,
        in_specs=[HBM, VMEM, VMEM, VMEM],
        out_specs=(HBM,) * 2,
        scratch_shapes=[
            pltpu.SMEM(wanted.shape, jnp.int32),
            pltpu.VMEM((per_device + 1,) + tile, jnp.float32),
            owned, owned, dma, dma((2, BLOCKS)),
        ],
        compiler_params=params(16),
        name="update",
    )(wanted, returned, velocity, accumulated)


def solution(mesh):
    split_shots = ("groups", "shot")
    return jax.shard_map(
        body,
        mesh=mesh,
        in_specs=(
            P(split_shots, None, None),
            P(split_shots, None, None),
            P(split_shots, None),
            P(split_shots),
            P(split_shots, None),
            P(split_shots, None, None, None, None),
            P(split_shots, None),
            P(split_shots, None, None),
        ),
        out_specs=(P(split_shots, None, None), P(split_shots, None, None)),
        check_vma=False,
    )
```

```python
import functools

import jax
import jax.numpy as jnp
import numpy as np
from jax import lax
from jax.experimental import pallas as pl
from jax.experimental.pallas import tpu as pltpu
from jax.sharding import PartitionSpec as P

TS = 16
AX = 2
AY = 2
AZ = 8
BX = AX * TS
BY = AY * TS
APT = AX * AY * AZ
ROWS = BX * AZ
LANES = BY * TS
HALF = TS * TS
BLOCKS = 8
GROUPS = 4
HELD = 2**16

scaled_weights = (-14350.0, 8064.0, -1008.0, 128.0, -9.0)
weight_scale = 1.0 / 5040.0
step_rate = 0.02


def stencil_matrices():
    lane = np.arange(LANES)
    y, l = lane // TS, lane % TS
    same = np.zeros((LANES, LANES), np.float32)
    cross = np.zeros((LANES, LANES), np.float32)
    for offset in range(1, 5):
        w = scaled_weights[offset]
        dy = np.abs(y[:, None] - y[None, :])
        dl = np.abs(l[:, None] - l[None, :])
        same += w * ((dl == 0) & (dy == offset))
        same += w * ((dy == 0) & (dl == offset))
        cross += w * ((dy == 0) & (dl == TS - offset))
    row = np.arange(ROWS)
    x, kz = row // (AZ * TS) * TS + row % TS, row // TS % AZ
    down = np.zeros((ROWS, ROWS), np.float32)
    for offset in range(1, 5):
        distance = np.abs(x[:, None] - x[None, :])
        down += scaled_weights[offset] * ((kz[:, None] == kz[None, :]) & (distance == offset))
    return same, np.concatenate([cross[:HALF, :HALF], down], axis=0)


def split(value):
    high = value.astype(jnp.bfloat16)
    rest = value - high.astype(jnp.float32)
    middle = rest.astype(jnp.bfloat16)
    low = (rest - middle.astype(jnp.float32)).astype(jnp.bfloat16)
    return high, middle, low


def stencil_products(field, parts, near, far, same_ref, cross_ref):
    for row in range(0, ROWS, 16):
        pieces = split(field[row : row + 16, :])
        for p in range(2):
            parts[p, row : row + 16, :] = pieces[p]
    same = same_ref[...]
    cross = cross_ref[:HALF, :]
    down = cross_ref[HALF:, :]
    dot = functools.partial(jnp.dot, preferred_element_type=jnp.float32)
    near[...] = dot(parts[0], same) + dot(parts[1], same)
    near[...] += dot(down, parts[0]) + dot(down, parts[1])
    for side in range(0, LANES, HALF):
        cols = slice(side, side + HALF)
        far[:, cols] = dot(parts[0, :, cols], cross) + dot(parts[1, :, cols], cross)


def laplacian_rows(field, near, far, row, upper):
    total = near[row : row + 8, :] + 3.0 * scaled_weights[0] * field[row : row + 8, :]
    kz = row // TS % AZ
    zero = jnp.zeros((8, LANES), jnp.float32)
    after = far[row + TS : row + TS + 8, :] if kz < AZ - 1 else zero
    before = far[row - TS : row - TS + 8, :] if kz > 0 else zero
    return weight_scale * (total + jnp.where(upper, after, before))


def upper_half():
    return lax.broadcasted_iota(jnp.int32, (8, LANES), 1) % TS >= TS // 2


def tile_row(x, z):
    return (x // TS * AZ + z // TS) * TS + x % TS


def slot_of(capacity, per_device, ids, k, counts):
    tile = ids[0, k]
    owner = tile // per_device
    rank = counts[owner]
    counts[owner] = rank + 1
    return owner * capacity + rank, tile - owner * per_device


def request_kernel(capacity, per_device, ids, table, counts):
    devices = table.shape[0]
    for owner in range(devices):
        counts[owner] = 0
    owner_of = lax.broadcasted_iota(jnp.int32, table.shape, 0)
    rank_of = lax.broadcasted_iota(jnp.int32, table.shape, 1)
    position = owner_of * capacity + jnp.where(rank_of < capacity, rank_of, -devices * capacity)
    found = jnp.full(table.shape, -1, jnp.int32)
    for k in range(APT):
        slot, tile = slot_of(capacity, per_device, ids, k, counts)
        found = jnp.where(position == slot, tile, found)
    table[...] = found


def gather_kernel(capacity, wanted_in, velocity, outgoing, wanted, owned, held, fetched, sent):
    devices = wanted_in.shape[0]
    listed = pltpu.make_async_copy(wanted_in, wanted, fetched.at[GROUPS])
    listed.start()
    tiles = velocity.shape[0] // GROUPS
    copies = [
        pltpu.make_async_copy(
            velocity.at[g * tiles : (g + 1) * tiles], owned.at[g * tiles : (g + 1) * tiles], fetched.at[g]
        )
        for g in range(GROUPS)
    ]
    for copy in copies:
        copy.start()
    listed.wait()
    for copy in copies:
        copy.wait()
    shots = devices // GROUPS
    copies = []
    for g in range(GROUPS):

        def step(shot, carry):
            for rank in range(capacity):
                held[shot * capacity + rank] = owned[jnp.maximum(wanted[shot, rank], 0)]
            return carry

        lax.fori_loop(g * shots, (g + 1) * shots, step, 0, unroll=True)
        part = slice(g * shots * capacity, (g + 1) * shots * capacity)
        copies.append(pltpu.make_async_copy(held.at[part], outgoing.at[part], sent.at[g]))
        copies[-1].start()
    for copy in copies:
        copy.wait()


def turn(start, step, x, y):
    group = lax.broadcasted_iota(jnp.int32, (8, 128), 1) // TS
    held = [start[step, pl.ds(x * BY + y + j, 8, BY), :] for j in range(8)]
    for bit in (1, 2, 4):
        low = (group & bit) == 0
        for j in range(8):
            if j & bit == 0:
                one, two = held[j], held[j + bit]
                held[j] = jnp.where(low, one, pltpu.roll(two, bit * TS, 1))
                held[j + bit] = jnp.where(low, pltpu.roll(one, 128 - bit * TS, 1), two)
    return held


def local_kernel(
    capacity, per_device, cells, recorded, ids, source, wavelet, start_in, same_ref, cross_ref,
    fields_out, slots_out, same_out, cross_out,
    start, lap0, base1, base2, current, parts, near, far, left, right, total, slots, counts, done,
):
    step = pl.program_id(0)
    last = pl.num_programs(0) - 1
    chunk = left.shape[1]

    def copy_of(n, held, target):
        return pltpu.make_async_copy(held, target, done.at[n])

    lists = [
        copy_of(0, slots, slots_out.at[:1]),
        copy_of(1, same_ref, same_out.at[:LANES]),
        copy_of(2, cross_ref, cross_out.at[: HALF + ROWS]),
    ]
    bases = [copy_of(3, base1, fields_out.at[ROWS : 2 * ROWS])]
    results = [
        copy_of(4, total.at[: 3 * ROWS], fields_out.at[2 * ROWS : 5 * ROWS]),
        copy_of(5, lap0, fields_out.at[:ROWS]),
    ]

    @pl.when(step == 0)
    def _():
        copies = [copy_of(6 + n, start_in.at[n], start.at[n, : BX * BY]) for n in range(2)]
        for copy in copies:
            copy.start()
        total[...] = jnp.zeros_like(total)
        for owner in range(counts.shape[0]):
            counts[owner] = 0
        for k in range(APT):
            slots[0, k], _ = slot_of(capacity, per_device, ids, k, counts)
        for copy in lists:
            copy.start()
        for copy in copies:
            copy.wait()

    @pl.when(step < last)
    def _():
        here = pl.ds(pl.multiple_of(step * chunk, chunk), chunk)
        cell = cells[:, here]
        x, y, z = cell // (BY * AZ * TS), (cell // (AZ * TS)) % BY, cell % (AZ * TS)
        row = tile_row(x, z)
        lane = y * TS + z % TS
        for at in range(0, LANES, 16):
            numbers = lax.broadcasted_iota(jnp.int32, (16, chunk), 0) + at
            right[at : at + 16, :] = jnp.where(numbers == lane, 1.0, 0.0).astype(jnp.bfloat16)
        pieces = []
        for n in range(2):
            pieces += split(jnp.broadcast_to(recorded[n : n + 1, here], (16, chunk)))
        for at in range(0, ROWS, 16):
            numbers = lax.broadcasted_iota(jnp.int32, (16, chunk), 0) + at
            hot = jnp.where(numbers == row, 1.0, 0.0).astype(jnp.bfloat16)
            left[at : at + 16, :] = hot
            for p in range(6):
                left[(p + 1) * ROWS + at : (p + 1) * ROWS + at + 16, :] = hot * pieces[p]
        total[...] += lax.dot_general(
            left[...], right[...], (((1,), (1,)), ((), ())), preferred_element_type=jnp.float32
        )

        cell = source[0]
        sx, sy, sz = cell // (BY * AZ * TS), (cell // (AZ * TS)) % BY, cell % (AZ * TS)
        source_row = tile_row(sx, sz)
        source_lane = sy * TS + sz % TS
        place = lax.broadcasted_iota(jnp.int32, (8, LANES), 0) * LANES + lax.broadcasted_iota(
            jnp.int32, (8, LANES), 1
        )
        first = step * 8
        old = [turn(start, 0, first, y) for y in range(0, BY, 8)]
        new = [turn(start, 1, first, y) for y in range(0, BY, 8)]
        for kz in range(AZ):
            at = pl.multiple_of((first // TS * AZ + kz) * TS + first % TS, 8)
            hit = place == (source_row - at) * LANES + source_lane
            rows = pl.ds(at, 8)
            now = jnp.concatenate([part[kz] for part in new], axis=1)
            before = jnp.concatenate([part[kz] for part in old], axis=1)
            current[rows, :] = now
            base1[rows, :] = 2.0 * now - before + jnp.where(hit, wavelet[0, 0], 0.0)
            base2[rows, :] = jnp.where(hit, wavelet[0, 1], 0.0) - now

    @pl.when(step == last)
    def _():
        for copy in bases:
            copy.start()

        def part(n):
            return total[n * ROWS : (n + 1) * ROWS, :]

        total[ROWS : 2 * ROWS, :] = part(1) + part(2) + part(3)
        total[2 * ROWS : 3 * ROWS, :] = part(0) * base2[...] - (part(4) + part(5) + part(6))
        results[0].start()
        stencil_products(current, parts, near, far, same_ref, cross_ref)
        upper = upper_half()
        for row in range(0, ROWS, 8):
            lap0[row : row + 8, :] = laplacian_rows(current, near, far, row, upper)
        results[1].start()
        for copy in lists + bases + results:
            copy.wait()


def gradient_kernel(
    arrived, fields_in, slots_in, same_in, cross_in, outgoing,
    slots, same_ref, cross_ref, lap0, base1, counts, sums0, known1,
    courant, field1, field2, partial, parts, near, far, done,
):
    inputs = [(slots_in.at[:1], slots)]
    inputs += [
        (fields_in.at[n * ROWS : (n + 1) * ROWS], target)
        for n, target in enumerate((lap0, base1, counts, sums0, known1))
    ]
    inputs += [(same_in.at[:LANES], same_ref), (cross_in.at[: HALF + ROWS], cross_ref)]
    copies = [pltpu.make_async_copy(a, b, done.at[n]) for n, (a, b) in enumerate(inputs)]
    for n in (0, 1, 2, 6, 7, 3, 5, 4):
        copies[n].start()
    copies[0].wait()
    copies[1].wait()
    copies[2].wait()
    for k in range(APT):
        kx, ky, kz = k // (AY * AZ), (k // AZ) % AY, k % AZ
        rows = slice((kx * AZ + kz) * TS, (kx * AZ + kz + 1) * TS)
        cols = slice(ky * HALF, (ky + 1) * HALF)
        speed = arrived[slots[0, k]]
        courant[rows, cols] = speed
        field1[rows, cols] = base1[rows, cols] + speed * speed * lap0[rows, cols]
    copies[6].wait()
    copies[7].wait()
    stencil_products(field1, parts, near, far, same_ref, cross_ref)
    upper = upper_half()
    for copy in copies[3:6]:
        copy.wait()
    for row in range(0, ROWS, 8):
        rows = slice(row, row + 8)
        speed = courant[rows, :]
        squared = speed * speed
        bent = laplacian_rows(field1, near, far, row, upper)
        miss2 = counts[rows, :] * (2.0 * field1[rows, :] + squared * bent) + known1[rows, :]
        field2[rows, :] = squared * miss2
        base = counts[rows, :] * field1[rows, :] - sums0[rows, :] + 2.0 * miss2
        partial[rows, :] = miss2 * bent + base * lap0[rows, :]
    stencil_products(field2, parts, near, far, same_ref, cross_ref)
    for kx in range(AX):
        for kz in range(AZ):
            for half in range(0, TS, 8):
                row = (kx * AZ + kz) * TS + half
                rows = slice(row, row + 8)
                bent = laplacian_rows(field2, near, far, row, upper)
                result = 2.0 * courant[rows, :] * (partial[rows, :] + bent * lap0[rows, :])
                for ky in range(AY):
                    slot = slots[0, (kx * AY + ky) * AZ + kz]
                    outgoing[slot, half : half + 8, :] = result[:, ky * HALF : (ky + 1) * HALF]


def update_kernel(
    capacity, wanted_in, returned, velocity, accumulated, velocity_out, accumulated_out,
    wanted, pooled, new_velocity, new_accumulated, listed, done,
):
    devices = wanted.shape[0]
    tiles = velocity.shape[0]
    copy = pltpu.make_async_copy(wanted_in, wanted, listed)
    copy.start()
    zero = jnp.zeros(pooled.shape[1:], jnp.float32)
    for tile in range(tiles):
        pooled[tile] = zero
    copy.wait()

    def add(shot, carry):
        for rank in range(capacity):
            tile = wanted[shot, rank]
            tile = jnp.where(tile < 0, tiles, tile)
            pooled[tile] += returned[shot * capacity + rank]
        return carry

    lax.fori_loop(0, devices, add, 0, unroll=8)
    block = tiles // BLOCKS
    copies = []
    for n in range(BLOCKS):
        here = slice(n * block, (n + 1) * block)
        gradient = pooled[here]
        total = accumulated[here] + gradient * gradient
        new_accumulated[here] = total
        new_velocity[here] = velocity[here] - step_rate * gradient * lax.rsqrt(total)
        for which, (source, target) in enumerate(((new_velocity, velocity_out), (new_accumulated, accumulated_out))):
            copies.append(pltpu.make_async_copy(source.at[here], target.at[here], done.at[which, n]))
            copies[-1].start()
    for copy in copies:
        copy.wait()


VMEM = pl.BlockSpec(memory_space=pltpu.VMEM)
HBM = pl.BlockSpec(memory_space=pltpu.HBM)
SMEM = pl.BlockSpec(memory_space=pltpu.SMEM)
MIB = 2**20


def params(mib):
    return pltpu.CompilerParams(vmem_limit_bytes=mib * MIB)


def f32(*shape):
    return jax.ShapeDtypeStruct(shape, jnp.float32)


def body(velocity, accumulated, aperture_tiles, source_cell, wavelet, start_field, receiver_cells, observed):
    devices = lax.axis_size("shot")
    per_device = velocity.shape[0]
    capacity = max(2, 2 * APT // devices)
    same, cross = stencil_matrices()
    same = jnp.asarray(same, jnp.bfloat16)
    cross = jnp.asarray(cross, jnp.bfloat16)

    table = pl.pallas_call(
        functools.partial(request_kernel, capacity, per_device),
        out_shape=jax.ShapeDtypeStruct((devices, 128), jnp.int32),
        in_specs=[SMEM],
        out_specs=VMEM,
        scratch_shapes=[pltpu.SMEM((devices,), jnp.int32)],
        name="requests",
    )(aperture_tiles)
    wanted = lax.all_to_all(table, "shot", split_axis=0, concat_axis=0, tiled=True)

    fields = (ROWS, LANES)
    whole = pltpu.VMEM(fields, jnp.float32)
    pieces = pltpu.VMEM((2,) + fields, jnp.bfloat16)
    dma = pltpu.SemaphoreType.DMA
    slots_total = devices * capacity
    held = pltpu.VMEM((slots_total,) + velocity.shape[1:], jnp.float32)
    owned = pltpu.VMEM(velocity.shape, jnp.float32)
    outgoing = pl.pallas_call(
        functools.partial(gather_kernel, capacity),
        out_shape=f32(slots_total, *velocity.shape[1:]),
        in_specs=[HBM, HBM],
        out_specs=HBM,
        scratch_shapes=[pltpu.SMEM(wanted.shape, jnp.int32), owned, held, dma((GROUPS + 1,)), dma((GROUPS,))],
        compiler_params=params(62),
        name="gather",
    )(wanted, velocity)
    arrived = lax.all_to_all(outgoing, "shot", split_axis=0, concat_axis=0, tiled=True)

    chunk = receiver_cells.shape[1] // (BX // 8)
    list_memory = pltpu.SMEM((1, 128), jnp.int32)
    held_bytes = HELD * 128 * 4
    constants = [pltpu.VMEM(same.shape, same.dtype), pltpu.VMEM(cross.shape, cross.dtype)]
    fields_held, slots_held, same_held, cross_held = pl.pallas_call(
        functools.partial(local_kernel, capacity, per_device),
        out_shape=(
            f32(held_bytes // (4 * LANES), LANES),
            jax.ShapeDtypeStruct((held_bytes // (4 * 128), 128), jnp.int32),
            jax.ShapeDtypeStruct((held_bytes // (2 * LANES), LANES), jnp.bfloat16),
            jax.ShapeDtypeStruct((held_bytes // (2 * HALF), HALF), jnp.bfloat16),
        ),
        grid=(BX // 8 + 1,),
        in_specs=[VMEM, VMEM, SMEM, SMEM, SMEM, HBM, VMEM, VMEM],
        out_specs=(HBM,) * 4,
        scratch_shapes=[
            pltpu.VMEM((2, BX * BY + 8 * BY, AZ * TS), jnp.float32),
            whole, whole, whole, whole, pieces, whole, whole,
            pltpu.VMEM((7 * ROWS, chunk), jnp.bfloat16),
            pltpu.VMEM((LANES, chunk), jnp.bfloat16),
            pltpu.VMEM((7 * ROWS, LANES), jnp.float32),
            list_memory,
            pltpu.SMEM((devices,), jnp.int32),
            dma((8,)),
        ],
        compiler_params=params(62),
        cost_estimate=pl.CostEstimate(flops=16 * 10**9, bytes_accessed=4 * MIB, transcendentals=0),
        name="local",
    )(
        receiver_cells, observed[0], aperture_tiles, source_cell, wavelet,
        start_field.reshape(2, BX * BY, AZ * TS), same, cross,
    )

    outgoing_gradient = pl.pallas_call(
        gradient_kernel,
        out_shape=f32(slots_total, *velocity.shape[1:]),
        in_specs=[VMEM, HBM, HBM, HBM, HBM],
        out_specs=VMEM,
        scratch_shapes=[
            list_memory, *constants, whole, whole, whole, whole, whole,
            whole, whole, whole, whole, pieces, whole, whole, dma((8,)),
        ],
        compiler_params=params(40),
        name="gradient",
    )(arrived, fields_held, slots_held, same_held, cross_held)
    returned = lax.all_to_all(outgoing_gradient, "shot", split_axis=0, concat_axis=0, tiled=True)

    tile = velocity.shape[1:]
    return pl.pallas_call(
        functools.partial(update_kernel, capacity),
        out_shape=(f32(*velocity.shape),) * 2,
        in_specs=[HBM, VMEM, VMEM, VMEM],
        out_specs=(HBM,) * 2,
        scratch_shapes=[
            pltpu.SMEM(wanted.shape, jnp.int32),
            pltpu.VMEM((per_device + 1,) + tile, jnp.float32),
            owned, owned, dma, dma((2, BLOCKS)),
        ],
        compiler_params=params(16),
        name="update",
    )(wanted, returned, velocity, accumulated)


def solution(mesh):
    split_shots = ("groups", "shot")
    return jax.shard_map(
        body,
        mesh=mesh,
        in_specs=(
            P(split_shots, None, None),
            P(split_shots, None, None),
            P(split_shots, None),
            P(split_shots),
            P(split_shots, None),
            P(split_shots, None, None, None, None),
            P(split_shots, None),
            P(split_shots, None, None),
        ),
        out_specs=(P(split_shots, None, None), P(split_shots, None, None)),
        check_vma=False,
    )
```

```python
import functools

import jax
import jax.numpy as jnp
import numpy as np
from jax import lax
from jax.experimental import pallas as pl
from jax.experimental.pallas import tpu as pltpu
from jax.sharding import PartitionSpec as P

TS = 16
AX = 2
AY = 2
AZ = 8
BX = AX * TS
BY = AY * TS
APT = AX * AY * AZ
ROWS = BX * AZ
LANES = BY * TS
HALF = TS * TS
BLOCKS = 4
GROUPS = 2
HELD = 2**16

scaled_weights = (-14350.0, 8064.0, -1008.0, 128.0, -9.0)
weight_scale = 1.0 / 5040.0
step_rate = 0.02


def stencil_matrices():
    lane = np.arange(LANES)
    y, l = lane // TS, lane % TS
    same = np.zeros((LANES, LANES), np.float32)
    cross = np.zeros((LANES, LANES), np.float32)
    for offset in range(1, 5):
        w = scaled_weights[offset]
        dy = np.abs(y[:, None] - y[None, :])
        dl = np.abs(l[:, None] - l[None, :])
        same += w * ((dl == 0) & (dy == offset))
        same += w * ((dy == 0) & (dl == offset))
        cross += w * ((dy == 0) & (dl == TS - offset))
    row = np.arange(ROWS)
    x, kz = row // (AZ * TS) * TS + row % TS, row // TS % AZ
    down = np.zeros((ROWS, ROWS), np.float32)
    for offset in range(1, 5):
        distance = np.abs(x[:, None] - x[None, :])
        down += scaled_weights[offset] * ((kz[:, None] == kz[None, :]) & (distance == offset))
    return same, np.concatenate([cross[:HALF, :HALF], down], axis=0)


def split(value):
    high = value.astype(jnp.bfloat16)
    rest = value - high.astype(jnp.float32)
    middle = rest.astype(jnp.bfloat16)
    low = (rest - middle.astype(jnp.float32)).astype(jnp.bfloat16)
    return high, middle, low


def stencil_products(field, parts, near, far, same_ref, cross_ref):
    for row in range(0, ROWS, 16):
        pieces = split(field[row : row + 16, :])
        for p in range(2):
            parts[p, row : row + 16, :] = pieces[p]
    same = same_ref[...]
    cross = cross_ref[:HALF, :]
    down = cross_ref[HALF:, :]
    dot = functools.partial(jnp.dot, preferred_element_type=jnp.float32)
    near[...] = dot(parts[0], same) + dot(parts[1], same)
    near[...] += dot(down, parts[0]) + dot(down, parts[1])
    for side in range(0, LANES, HALF):
        cols = slice(side, side + HALF)
        far[:, cols] = dot(parts[0, :, cols], cross) + dot(parts[1, :, cols], cross)


def laplacian_rows(field, near, far, row, upper):
    total = near[row : row + 8, :] + 3.0 * scaled_weights[0] * field[row : row + 8, :]
    kz = row // TS % AZ
    zero = jnp.zeros((8, LANES), jnp.float32)
    after = far[row + TS : row + TS + 8, :] if kz < AZ - 1 else zero
    before = far[row - TS : row - TS + 8, :] if kz > 0 else zero
    return weight_scale * (total + jnp.where(upper, after, before))


def upper_half():
    return lax.broadcasted_iota(jnp.int32, (8, LANES), 1) % TS >= TS // 2


def tile_row(x, z):
    return (x // TS * AZ + z // TS) * TS + x % TS


def slot_of(capacity, per_device, ids, k, counts):
    tile = ids[0, k]
    owner = tile // per_device
    rank = counts[owner]
    counts[owner] = rank + 1
    return owner * capacity + rank, tile - owner * per_device


def request_kernel(capacity, per_device, ids, table, counts):
    devices = table.shape[0]
    for owner in range(devices):
        counts[owner] = 0
    owner_of = lax.broadcasted_iota(jnp.int32, table.shape, 0)
    rank_of = lax.broadcasted_iota(jnp.int32, table.shape, 1)
    position = owner_of * capacity + jnp.where(rank_of < capacity, rank_of, -devices * capacity)
    found = jnp.full(table.shape, -1, jnp.int32)
    for k in range(APT):
        slot, tile = slot_of(capacity, per_device, ids, k, counts)
        found = jnp.where(position == slot, tile, found)
    table[...] = found


def gather_kernel(capacity, wanted_in, velocity, outgoing, wanted, owned, held, fetched, sent):
    devices = wanted_in.shape[0]
    listed = pltpu.make_async_copy(wanted_in, wanted, fetched.at[GROUPS])
    listed.start()
    tiles = velocity.shape[0] // GROUPS
    copies = [
        pltpu.make_async_copy(
            velocity.at[g * tiles : (g + 1) * tiles], owned.at[g * tiles : (g + 1) * tiles], fetched.at[g]
        )
        for g in range(GROUPS)
    ]
    for copy in copies:
        copy.start()
    listed.wait()
    for copy in copies:
        copy.wait()
    shots = devices // GROUPS
    copies = []
    for g in range(GROUPS):

        def step(shot, carry):
            for rank in range(capacity):
                held[shot * capacity + rank] = owned[jnp.maximum(wanted[shot, rank], 0)]
            return carry

        lax.fori_loop(g * shots, (g + 1) * shots, step, 0, unroll=True)
        part = slice(g * shots * capacity, (g + 1) * shots * capacity)
        copies.append(pltpu.make_async_copy(held.at[part], outgoing.at[part], sent.at[g]))
        copies[-1].start()
    for copy in copies:
        copy.wait()


def turn(start, step, x, y):
    group = lax.broadcasted_iota(jnp.int32, (8, 128), 1) // TS
    held = [start[step, pl.ds(x * BY + y + j, 8, BY), :] for j in range(8)]
    for bit in (1, 2, 4):
        low = (group & bit) == 0
        for j in range(8):
            if j & bit == 0:
                one, two = held[j], held[j + bit]
                held[j] = jnp.where(low, one, pltpu.roll(two, bit * TS, 1))
                held[j + bit] = jnp.where(low, pltpu.roll(one, 128 - bit * TS, 1), two)
    return held


def local_kernel(
    capacity, per_device, cells, recorded, ids, source, wavelet, start_in, same_ref, cross_ref,
    fields_out, slots_out, same_out, cross_out,
    start, lap0, base1, base2, current, parts, near, far, left, right, total, slots, counts, done,
):
    step = pl.program_id(0)
    last = pl.num_programs(0) - 1
    chunk = left.shape[1]

    def copy_of(n, held, target):
        return pltpu.make_async_copy(held, target, done.at[n])

    lists = [
        copy_of(0, slots, slots_out.at[:1]),
        copy_of(1, same_ref, same_out.at[:LANES]),
        copy_of(2, cross_ref, cross_out.at[: HALF + ROWS]),
    ]
    bases = [copy_of(3, base1, fields_out.at[ROWS : 2 * ROWS])]
    results = [
        copy_of(4, total.at[: 3 * ROWS], fields_out.at[2 * ROWS : 5 * ROWS]),
        copy_of(5, lap0, fields_out.at[:ROWS]),
    ]

    @pl.when(step == 0)
    def _():
        copies = [copy_of(6 + n, start_in.at[n], start.at[n, : BX * BY]) for n in range(2)]
        for copy in copies:
            copy.start()
        total[...] = jnp.zeros_like(total)
        for owner in range(counts.shape[0]):
            counts[owner] = 0
        for k in range(APT):
            slots[0, k], _ = slot_of(capacity, per_device, ids, k, counts)
        for copy in lists:
            copy.start()
        for copy in copies:
            copy.wait()

    @pl.when(step < last)
    def _():
        here = pl.ds(pl.multiple_of(step * chunk, chunk), chunk)
        cell = cells[:, here]
        x, y, z = cell // (BY * AZ * TS), (cell // (AZ * TS)) % BY, cell % (AZ * TS)
        row = tile_row(x, z)
        lane = y * TS + z % TS
        for at in range(0, LANES, 16):
            numbers = lax.broadcasted_iota(jnp.int32, (16, chunk), 0) + at
            right[at : at + 16, :] = jnp.where(numbers == lane, 1.0, 0.0).astype(jnp.bfloat16)
        pieces = []
        for n in range(2):
            pieces += split(jnp.broadcast_to(recorded[n : n + 1, here], (16, chunk)))
        for at in range(0, ROWS, 16):
            numbers = lax.broadcasted_iota(jnp.int32, (16, chunk), 0) + at
            hot = jnp.where(numbers == row, 1.0, 0.0).astype(jnp.bfloat16)
            left[at : at + 16, :] = hot
            for p in range(6):
                left[(p + 1) * ROWS + at : (p + 1) * ROWS + at + 16, :] = hot * pieces[p]
        total[...] += lax.dot_general(
            left[...], right[...], (((1,), (1,)), ((), ())), preferred_element_type=jnp.float32
        )

        cell = source[0]
        sx, sy, sz = cell // (BY * AZ * TS), (cell // (AZ * TS)) % BY, cell % (AZ * TS)
        source_row = tile_row(sx, sz)
        source_lane = sy * TS + sz % TS
        place = lax.broadcasted_iota(jnp.int32, (8, LANES), 0) * LANES + lax.broadcasted_iota(
            jnp.int32, (8, LANES), 1
        )
        first = step * 8
        old = [turn(start, 0, first, y) for y in range(0, BY, 8)]
        new = [turn(start, 1, first, y) for y in range(0, BY, 8)]
        for kz in range(AZ):
            at = pl.multiple_of((first // TS * AZ + kz) * TS + first % TS, 8)
            hit = place == (source_row - at) * LANES + source_lane
            rows = pl.ds(at, 8)
            now = jnp.concatenate([part[kz] for part in new], axis=1)
            before = jnp.concatenate([part[kz] for part in old], axis=1)
            current[rows, :] = now
            base1[rows, :] = 2.0 * now - before + jnp.where(hit, wavelet[0, 0], 0.0)
            base2[rows, :] = jnp.where(hit, wavelet[0, 1], 0.0) - now

    @pl.when(step == last)
    def _():
        for copy in bases:
            copy.start()

        def part(n):
            return total[n * ROWS : (n + 1) * ROWS, :]

        total[ROWS : 2 * ROWS, :] = part(1) + part(2) + part(3)
        total[2 * ROWS : 3 * ROWS, :] = part(0) * base2[...] - (part(4) + part(5) + part(6))
        results[0].start()
        stencil_products(current, parts, near, far, same_ref, cross_ref)
        upper = upper_half()
        for row in range(0, ROWS, 8):
            lap0[row : row + 8, :] = laplacian_rows(current, near, far, row, upper)
        results[1].start()
        for copy in lists + bases + results:
            copy.wait()


def gradient_kernel(
    arrived, fields_in, slots_in, same_in, cross_in, outgoing,
    slots, same_ref, cross_ref, lap0, base1, counts, sums0, known1,
    courant, field1, field2, partial, parts, near, far, done,
):
    inputs = [(slots_in.at[:1], slots)]
    inputs += [
        (fields_in.at[n * ROWS : (n + 1) * ROWS], target)
        for n, target in enumerate((lap0, base1, counts, sums0, known1))
    ]
    inputs += [(same_in.at[:LANES], same_ref), (cross_in.at[: HALF + ROWS], cross_ref)]
    copies = [pltpu.make_async_copy(a, b, done.at[n]) for n, (a, b) in enumerate(inputs)]
    for n in (0, 1, 2, 6, 7, 3, 5, 4):
        copies[n].start()
    copies[0].wait()
    copies[1].wait()
    copies[2].wait()
    for k in range(APT):
        kx, ky, kz = k // (AY * AZ), (k // AZ) % AY, k % AZ
        rows = slice((kx * AZ + kz) * TS, (kx * AZ + kz + 1) * TS)
        cols = slice(ky * HALF, (ky + 1) * HALF)
        speed = arrived[slots[0, k]]
        courant[rows, cols] = speed
        field1[rows, cols] = base1[rows, cols] + speed * speed * lap0[rows, cols]
    copies[6].wait()
    copies[7].wait()
    stencil_products(field1, parts, near, far, same_ref, cross_ref)
    upper = upper_half()
    for copy in copies[3:6]:
        copy.wait()
    for row in range(0, ROWS, 8):
        rows = slice(row, row + 8)
        speed = courant[rows, :]
        squared = speed * speed
        bent = laplacian_rows(field1, near, far, row, upper)
        miss2 = counts[rows, :] * (2.0 * field1[rows, :] + squared * bent) + known1[rows, :]
        field2[rows, :] = squared * miss2
        base = counts[rows, :] * field1[rows, :] - sums0[rows, :] + 2.0 * miss2
        partial[rows, :] = miss2 * bent + base * lap0[rows, :]
    stencil_products(field2, parts, near, far, same_ref, cross_ref)
    for kx in range(AX):
        for kz in range(AZ):
            for half in range(0, TS, 8):
                row = (kx * AZ + kz) * TS + half
                rows = slice(row, row + 8)
                bent = laplacian_rows(field2, near, far, row, upper)
                result = 2.0 * courant[rows, :] * (partial[rows, :] + bent * lap0[rows, :])
                for ky in range(AY):
                    slot = slots[0, (kx * AY + ky) * AZ + kz]
                    outgoing[slot, half : half + 8, :] = result[:, ky * HALF : (ky + 1) * HALF]


def update_kernel(
    capacity, wanted_in, returned, velocity, accumulated, velocity_out, accumulated_out,
    wanted, pooled, new_velocity, new_accumulated, listed, done,
):
    devices = wanted.shape[0]
    tiles = velocity.shape[0]
    copy = pltpu.make_async_copy(wanted_in, wanted, listed)
    copy.start()
    zero = jnp.zeros(pooled.shape[1:], jnp.float32)
    for tile in range(tiles):
        pooled[tile] = zero
    copy.wait()

    def add(shot, carry):
        for rank in range(capacity):
            tile = wanted[shot, rank]
            tile = jnp.where(tile < 0, tiles, tile)
            pooled[tile] += returned[shot * capacity + rank]
        return carry

    lax.fori_loop(0, devices, add, 0, unroll=8)
    block = tiles // BLOCKS
    copies = []
    for n in range(BLOCKS):
        here = slice(n * block, (n + 1) * block)
        gradient = pooled[here]
        total = accumulated[here] + gradient * gradient
        new_accumulated[here] = total
        new_velocity[here] = velocity[here] - step_rate * gradient * lax.rsqrt(total)
        for which, (source, target) in enumerate(((new_velocity, velocity_out), (new_accumulated, accumulated_out))):
            copies.append(pltpu.make_async_copy(source.at[here], target.at[here], done.at[which, n]))
            copies[-1].start()
    for copy in copies:
        copy.wait()


VMEM = pl.BlockSpec(memory_space=pltpu.VMEM)
HBM = pl.BlockSpec(memory_space=pltpu.HBM)
SMEM = pl.BlockSpec(memory_space=pltpu.SMEM)
MIB = 2**20


def params(mib):
    return pltpu.CompilerParams(vmem_limit_bytes=mib * MIB)


def f32(*shape):
    return jax.ShapeDtypeStruct(shape, jnp.float32)


def body(velocity, accumulated, aperture_tiles, source_cell, wavelet, start_field, receiver_cells, observed):
    devices = lax.axis_size("shot")
    per_device = velocity.shape[0]
    capacity = max(2, 2 * APT // devices)
    same, cross = stencil_matrices()
    same = jnp.asarray(same, jnp.bfloat16)
    cross = jnp.asarray(cross, jnp.bfloat16)

    table = pl.pallas_call(
        functools.partial(request_kernel, capacity, per_device),
        out_shape=jax.ShapeDtypeStruct((devices, 128), jnp.int32),
        in_specs=[SMEM],
        out_specs=VMEM,
        scratch_shapes=[pltpu.SMEM((devices,), jnp.int32)],
        name="requests",
    )(aperture_tiles)
    wanted = lax.all_to_all(table, "shot", split_axis=0, concat_axis=0, tiled=True)

    fields = (ROWS, LANES)
    whole = pltpu.VMEM(fields, jnp.float32)
    pieces = pltpu.VMEM((2,) + fields, jnp.bfloat16)
    dma = pltpu.SemaphoreType.DMA
    slots_total = devices * capacity
    held = pltpu.VMEM((slots_total,) + velocity.shape[1:], jnp.float32)
    owned = pltpu.VMEM(velocity.shape, jnp.float32)
    outgoing = pl.pallas_call(
        functools.partial(gather_kernel, capacity),
        out_shape=f32(slots_total, *velocity.shape[1:]),
        in_specs=[HBM, HBM],
        out_specs=HBM,
        scratch_shapes=[pltpu.SMEM(wanted.shape, jnp.int32), owned, held, dma((GROUPS + 1,)), dma((GROUPS,))],
        compiler_params=params(62),
        name="gather",
    )(wanted, velocity)
    arrived = lax.all_to_all(outgoing, "shot", split_axis=0, concat_axis=0, tiled=True)

    chunk = receiver_cells.shape[1] // (BX // 8)
    list_memory = pltpu.SMEM((1, 128), jnp.int32)
    held_bytes = HELD * 128 * 4
    constants = [pltpu.VMEM(same.shape, same.dtype), pltpu.VMEM(cross.shape, cross.dtype)]
    fields_held, slots_held, same_held, cross_held = pl.pallas_call(
        functools.partial(local_kernel, capacity, per_device),
        out_shape=(
            f32(held_bytes // (4 * LANES), LANES),
            jax.ShapeDtypeStruct((held_bytes // (4 * 128), 128), jnp.int32),
            jax.ShapeDtypeStruct((held_bytes // (2 * LANES), LANES), jnp.bfloat16),
            jax.ShapeDtypeStruct((held_bytes // (2 * HALF), HALF), jnp.bfloat16),
        ),
        grid=(BX // 8 + 1,),
        in_specs=[VMEM, VMEM, SMEM, SMEM, SMEM, HBM, VMEM, VMEM],
        out_specs=(HBM,) * 4,
        scratch_shapes=[
            pltpu.VMEM((2, BX * BY + 8 * BY, AZ * TS), jnp.float32),
            whole, whole, whole, whole, pieces, whole, whole,
            pltpu.VMEM((7 * ROWS, chunk), jnp.bfloat16),
            pltpu.VMEM((LANES, chunk), jnp.bfloat16),
            pltpu.VMEM((7 * ROWS, LANES), jnp.float32),
            list_memory,
            pltpu.SMEM((devices,), jnp.int32),
            dma((8,)),
        ],
        compiler_params=params(62),
        cost_estimate=pl.CostEstimate(flops=16 * 10**9, bytes_accessed=4 * MIB, transcendentals=0),
        name="local",
    )(
        receiver_cells, observed[0], aperture_tiles, source_cell, wavelet,
        start_field.reshape(2, BX * BY, AZ * TS), same, cross,
    )

    outgoing_gradient = pl.pallas_call(
        gradient_kernel,
        out_shape=f32(slots_total, *velocity.shape[1:]),
        in_specs=[VMEM, HBM, HBM, HBM, HBM],
        out_specs=VMEM,
        scratch_shapes=[
            list_memory, *constants, whole, whole, whole, whole, whole,
            whole, whole, whole, whole, pieces, whole, whole, dma((8,)),
        ],
        compiler_params=params(40),
        name="gradient",
    )(arrived, fields_held, slots_held, same_held, cross_held)
    returned = lax.all_to_all(outgoing_gradient, "shot", split_axis=0, concat_axis=0, tiled=True)

    tile = velocity.shape[1:]
    return pl.pallas_call(
        functools.partial(update_kernel, capacity),
        out_shape=(f32(*velocity.shape),) * 2,
        in_specs=[HBM, VMEM, VMEM, VMEM],
        out_specs=(HBM,) * 2,
        scratch_shapes=[
            pltpu.SMEM(wanted.shape, jnp.int32),
            pltpu.VMEM((per_device + 1,) + tile, jnp.float32),
            owned, owned, dma, dma((2, BLOCKS)),
        ],
        compiler_params=params(16),
        name="update",
    )(wanted, returned, velocity, accumulated)


def solution(mesh):
    split_shots = ("groups", "shot")
    return jax.shard_map(
        body,
        mesh=mesh,
        in_specs=(
            P(split_shots, None, None),
            P(split_shots, None, None),
            P(split_shots, None),
            P(split_shots),
            P(split_shots, None),
            P(split_shots, None, None, None, None),
            P(split_shots, None),
            P(split_shots, None, None),
        ),
        out_specs=(P(split_shots, None, None), P(split_shots, None, None)),
        check_vma=False,
    )
```
